32 devices in a mesh: blk: 8 (over y, x, core), head: 4 (over z).
Axes of the slice: x: 2, y: 2, z: 4, core: 2. Of those that a mesh axis runs over, the one named last changes fastest.
Arguments:
- tokens: bfloat16 [4096, 1024], P(('blk', 'head')), may hold values from -6 to 6
- out_grad: bfloat16 [4096, 1024], P(('blk', 'head')), may hold values from -6 to 6
- ln_gain: bfloat16 [1024], P(('blk', 'head')), may hold values from 0.5 to 1.5
- w_query: bfloat16 [1024, 512], P(('blk', 'head')), may hold values from -0.25 to 0.25
- w_key: bfloat16 [1024, 512], P(('blk', 'head')), may hold values from -0.25 to 0.25
- w_value: bfloat16 [1024, 2560], P(('blk', 'head')), may hold values from -0.1875 to 0.1875
- w_output: bfloat16 [2560, 1024], P(('blk', 'head')), may hold values from -3 to 3
- route_value: bfloat16 [1024, 20], P(('blk', 'head')), may hold values from -0.1875 to 0.1875
- route_output: bfloat16 [1024, 20], P(('blk', 'head')), may hold values from -0.1875 to 0.1875
- route_expert: bfloat16 [1024, 256], P(None, ('blk', 'head')), may hold values from -0.09375 to 0.09375
- w_up: bfloat16 [1024, 32768], P(None, ('blk', 'head')), may hold values from -0.1875 to 0.1875
- w_down: bfloat16 [32768, 1024], P(('blk', 'head')), may hold values from -0.5 to 0.5
- value_ids: int32 [4096, 4, 2], P(('blk', 'head')), may hold values from 0 to 4, all different within a row
- output_ids: int32 [4096, 4, 2], P(('blk', 'head')), may hold values from 0 to 4, all different within a row
- expert_ids: int32 [4096, 16], P(('blk', 'head')), may hold values from 0 to 255, all different within a row; in each aligned block of 128 rows (0 to 127, 128 to 255, ...) at most 10 rows name the same one
Outputs:
- layer_out: float32 [4096, 1024], P(('blk', 'head'))
- grad_tokens: float32 [4096, 1024], P(('blk', 'head'))
- grad_ln_gain: float32 [1024], P(('blk', 'head'))
- grad_w_query: float32 [1024, 512], P(('blk', 'head'))
- grad_w_key: float32 [1024, 512], P(('blk', 'head'))
- grad_w_value: float32 [1024, 2560], P(('blk', 'head'))
- grad_w_output: float32 [2560, 1024], P(('blk', 'head'))
- grad_route_value: float32 [1024, 20], P(('blk', 'head'))
- grad_route_output: float32 [1024, 20], P(('blk', 'head'))
- grad_route_expert: float32 [1024, 256], P(None, ('blk', 'head'))
- grad_w_up: float32 [1024, 32768], P(None, ('blk', 'head'))
- grad_w_down: float32 [32768, 1024], P(('blk', 'head'))
The draws below stay inside these ranges and needn't reach their ends.
Inputs may be any that keep to these rules, and one draw needn't show every extreme that they name: `expert_ids`: in the 128 tokens of each device no expert is named more than 10 times; each token names 16 different experts. `value_ids`: each token names 2 different value experts in each head. `output_ids`: each token names 2 different output experts in each head.
All inputs are finite; a program needn't handle non-finite values.
Results may differ from the reference program's by a relative error of at most 0.02.
Values may be sent and summed in bfloat16 or wider, within the bound.
No kernel may reach another device: no remote copies, remote signals or barrier semaphores. Data moves between devices by JAX's collectives and lax.ppermute only.
A program may use at most 192 MiB of HBM per device.

```python
import math
import jax
import jax.numpy as jnp
import numpy as np
from jax import lax

D = 1024
HEADS = 4
HEAD_DIM = 128
ATT_EXPERTS = 5
ATT_TOP = 2
EXPERTS = 256
EXPERT_WIDTH = 128
EXPERT_TOP = 16
ATT_BLOCK = 256
TOK_DEV = 128
CAPACITY = 10
SEQ = 4096


def level_of(rng, extent, pieces, smallest, largest):
    def one(axis_at, parts):
        heights = jax.random.uniform(jax.random.fold_in(jax.random.fold_in(rng, 6), axis_at), (parts,), jnp.float32, smallest / len(pieces), largest / len(pieces))
        return jnp.repeat(jnp.exp(heights), extent[axis_at] // parts).reshape((-1,) + (1,) * (len(extent) - axis_at - 1))

    loudness = one(*pieces[0])
    for cut in pieces[1:]:
        loudness = loudness * one(*cut)
    return loudness


def distinct(stream_key, rows, amount, top, lift):
    order = jax.random.permutation(jax.random.fold_in(stream_key, 1), amount)
    boost = order
    for power in range(3):
        boost = boost * boost // amount
    boost = boost * lift // amount
    chance = jax.random.randint(jax.random.fold_in(stream_key, 2), (rows, amount), 0, 4096) + boost
    fixed_rows = jax.random.permutation(jax.random.fold_in(stream_key, 3), rows)[jnp.arange(amount) % rows]
    chance = jnp.where(jnp.arange(rows)[:, None] == fixed_rows[None, :], 1 << 14, chance)
    merit = chance * amount + jnp.arange(amount)
    return lax.top_k(merit.astype(jnp.int32), top)[1].astype(jnp.int32)


def deal_out(rng, own, number, rows, amount, top, bound, skew):
    ranking = jax.random.permutation(rng, amount)
    packed, usual = shares(amount, rows * top, bound, skew, True), shares(amount, rows * top, bound, skew, False)
    places = jnp.arange(amount)

    def named(tallies, rotation):
        used = int((tallies > 0).sum())
        fixed = max(1, used // 4)
        moved = fixed + (places - fixed + rotation * (used - fixed)) % max(1, amount - fixed)
        return jnp.zeros((amount,), jnp.int32).at[ranking[jnp.where(places < fixed, places, moved)]].set(jnp.asarray(tallies, jnp.int32))

    tallies = jnp.where(number % 4 == 0, named(packed, number // 4), named(usual, number - number // 4 - 1))
    mixed = jax.random.permutation(jax.random.fold_in(own, 3), amount)
    donor, receiver = mixed[0:amount // 2 * 2:2], mixed[1:amount // 2 * 2:2]
    slack = jnp.minimum(tallies[donor] - 1, bound - tallies[receiver]) // 2
    slack = jnp.where((donor == ranking[0]) | (receiver == ranking[0]) | (tallies[receiver] == 0), 0, jnp.maximum(slack, 0))
    moved = jax.random.randint(jax.random.fold_in(own, 4), (amount // 2,), 0, 1 << 20) % (slack + 1)
    tallies = tallies.at[donor].add(-moved).at[receiver].add(moved)
    items = jnp.searchsorted(jnp.cumsum(tallies), jnp.arange(rows * top), side="right").astype(jnp.int32)
    grid = items.reshape(top, rows).T
    grid = grid[jax.random.permutation(jax.random.fold_in(own, 1), rows)]
    rotation = jax.random.randint(jax.random.fold_in(own, 2), (rows, 1), 0, top)
    return jnp.take_along_axis(grid, (jnp.arange(top)[None, :] + rotation) % top, axis=1)


def shares(count, total, bound, skew, full):
    weights = [(1 << 20) // math.isqrt(standing ** skew) + 1 for standing in range(1, count + 1)]
    largest = bound if full else min(bound, max(-(-total // count), total * weights[0] // sum(weights)))
    least = 1 if total - largest >= count - 1 else 0
    given, spare = [largest] + [least] * (count - 1), total - largest - least * (count - 1)
    while spare > 0:
        free = [i for i in range(1, count) if given[i] < largest] or [i for i in range(1, count) if given[i] < bound]
        mass, budget = sum([weights[i] for i in free]), spare
        for i in free:
            more = min(bound - given[i], max(1, budget * weights[i] // mass), spare)
            given[i] = given[i] + more
            spare = spare - more
    return np.array(given)


def scatter_about(key, shape, spread, bound, split=(), kind=jnp.bfloat16):
    array = spread * jax.random.normal(key, shape, jnp.float32)
    if split:
        array = array * level_of(key, shape, split, -0.22, 0.18)
    return jnp.clip(array, -bound, bound).astype(kind)


def setup_inputs(seed: int = 0) -> dict:
    key_of = jax.random.split(jax.random.key(seed), 16)
    tokens = scatter_about(key_of[0], (SEQ, D), 1.0, 6.0, ((0, 32),))
    out_grad = scatter_about(key_of[1], (SEQ, D), 1.0, 6.0, ((0, 32),))
    ln_gain = jnp.clip(1.0 + 0.1 * jax.random.normal(key_of[2], (D,), jnp.float32), 0.5, 1.5).astype(jnp.bfloat16)
    w_query = scatter_about(key_of[3], (D, HEADS * HEAD_DIM), (D // 2) ** -0.5, 0.25, ((0, 32),))
    w_key = scatter_about(key_of[4], (D, HEADS * HEAD_DIM), (D // 2) ** -0.5, 0.25, ((0, 32),))
    w_value = scatter_about(key_of[5], (D, HEADS * ATT_EXPERTS * HEAD_DIM), D ** -0.5, 0.1875, ((0, 32),))
    w_output = scatter_about(key_of[6], (HEADS * ATT_EXPERTS * HEAD_DIM, D), 4 ** -0.5, 3.0, ((0, 32),))
    route_value = scatter_about(key_of[7], (D, HEADS * ATT_EXPERTS), D ** -0.5, 0.1875, ((0, 32),))
    route_output = scatter_about(key_of[8], (D, HEADS * ATT_EXPERTS), D ** -0.5, 0.1875, ((0, 32),))
    route_expert = scatter_about(key_of[9], (D, EXPERTS), (4 * D) ** -0.5, 0.09375, ((1, 32),))
    w_up = scatter_about(key_of[10], (D, EXPERTS * EXPERT_WIDTH), D ** -0.5, 0.1875, ((1, 32),))
    w_down = scatter_about(key_of[11], (EXPERTS * EXPERT_WIDTH, D), EXPERT_WIDTH ** -0.5, 0.5, ((0, 32),))
    value_ids = distinct(key_of[12], SEQ * HEADS, ATT_EXPERTS, ATT_TOP, 0).reshape((SEQ, HEADS, ATT_TOP))
    output_ids = distinct(key_of[13], SEQ * HEADS, ATT_EXPERTS, ATT_TOP, 0).reshape((SEQ, HEADS, ATT_TOP))
    expert_ids_keys = jax.random.split(jax.random.fold_in(key_of[14], 1), SEQ // TOK_DEV)
    expert_ids_turns = jax.random.permutation(jax.random.fold_in(key_of[14], 3), SEQ // TOK_DEV)
    expert_ids = jax.vmap(lambda own, number: deal_out(jax.random.fold_in(key_of[14], 2), own, number, TOK_DEV, EXPERTS, EXPERT_TOP, CAPACITY, 1))(expert_ids_keys, expert_ids_turns).reshape((SEQ, EXPERT_TOP))
    return dict(tokens=tokens, out_grad=out_grad, ln_gain=ln_gain, w_query=w_query, w_key=w_key, w_value=w_value, w_output=w_output, route_value=route_value, route_output=route_output, route_expert=route_expert, w_up=w_up, w_down=w_down, value_ids=value_ids, output_ids=output_ids, expert_ids=expert_ids)


ln_eps = 1e-05
rope_base = 10000.0

@jax.custom_vjp
def low(v):
    return lax.optimization_barrier(v.astype(jnp.bfloat16)).astype(jnp.float32)

@jax.custom_vjp
def low_back(v):
    return v

def low_keep(v):
    return (low(v), None)

def low_pass(kept, grad):
    return (grad,)

def back_keep(v):
    return (v, None)

def back_low(kept, grad):
    return (low(grad),)
low.defvjp(low_keep, low_pass)
low_back.defvjp(back_keep, back_low)

def product(spec, left, right):
    return jnp.einsum(spec, left, right, precision=lax.Precision.HIGHEST)

def rotate(values, places, sign_value):
    half_size = values.shape[-1] // 2
    frequency = rope_base ** (-jnp.arange(half_size, dtype=jnp.float32) / half_size)
    angles = places.astype(jnp.float32)[:, None] * frequency[None, :]
    cosine = jnp.cos(angles)[:, None, :]
    sine_part = sign_value * jnp.sin(angles)[:, None, :]
    first_half = values[..., :half_size]
    second_half = values[..., half_size:]
    return jnp.concatenate([first_half * cosine - second_half * sine_part, second_half * cosine + first_half * sine_part], axis=-1)

def attend(queries, key_rows, values):
    seq_len = queries.shape[0]
    block_rows = min(1024, seq_len)
    block_total = seq_len // block_rows
    key_blocks = jnp.arange(seq_len, dtype=jnp.int32) // ATT_BLOCK
    score_scale = HEAD_DIM ** (-0.5)

    def one_block(element):
        query_rows, first_row = element
        raw_scores = low_back(product('qhd,khd->hqk', query_rows, key_rows)) * score_scale
        query_blocks = (first_row + jnp.arange(block_rows, dtype=jnp.int32)) // ATT_BLOCK
        allowed = key_blocks[None, :] <= query_blocks[:, None]
        masked = jnp.where(allowed[None], raw_scores, -jnp.inf)
        top_score = lax.optimization_barrier(jnp.max(masked, -1, keepdims=True))
        exponent = jnp.exp(masked - top_score)
        prob_full = exponent / lax.optimization_barrier(jnp.sum(exponent, -1, keepdims=True))
        return product('hqk,khd->qhd', low(prob_full), values)
    starts = jnp.arange(block_total, dtype=jnp.int32) * block_rows
    blocks_out = lax.map(jax.checkpoint(one_block), (queries.reshape(block_total, block_rows, HEADS, HEAD_DIM), starts))
    return blocks_out.reshape(seq_len, HEADS, HEAD_DIM)

def reference(tokens, out_grad, ln_gain, w_query, w_key, w_value, w_output, route_value, route_output, route_expert, w_up, w_down, value_ids, output_ids, expert_ids):
    value_hot = lax.optimization_barrier(jnp.sum((value_ids[..., None] == jnp.arange(ATT_EXPERTS, dtype=jnp.int32)).astype(jnp.float32), 2))
    output_hot = lax.optimization_barrier(jnp.sum((output_ids[..., None] == jnp.arange(ATT_EXPERTS, dtype=jnp.int32)).astype(jnp.float32), 2))
    expert_hot = lax.optimization_barrier(jnp.sum((expert_ids[..., None] == jnp.arange(EXPERTS, dtype=jnp.int32)).astype(jnp.float32), 1))

    def forward(inputs, gain, query_weight, key_weight, value_weight, output_weight, value_router, output_router, expert_router, up_weight, down_weight):
        seq_len = inputs.shape[0]
        places = jnp.arange(seq_len, dtype=jnp.int32)
        centre = lax.optimization_barrier(jnp.mean(inputs, -1, keepdims=True))
        shifted = inputs - centre
        inv_std = lax.rsqrt(lax.optimization_barrier(jnp.mean(shifted * shifted, -1, keepdims=True)) + ln_eps)
        normed = low(shifted * inv_std * gain)
        query_pre = low_back(product('td,dk->tk', normed, query_weight)).reshape(seq_len, HEADS, HEAD_DIM)
        key_pre = low_back(product('td,dk->tk', normed, key_weight)).reshape(seq_len, HEADS, HEAD_DIM)
        queries = low(rotate(query_pre, places, 1.0))
        key_rows = low(rotate(key_pre, places, 1.0))
        value_gate = jax.nn.sigmoid(low_back(product('td,dk->tk', inputs, value_router))).reshape(seq_len, HEADS, ATT_EXPERTS)
        expert_values = low_back(product('td,dk->tk', inputs, value_weight)).reshape(seq_len, HEADS, ATT_EXPERTS, HEAD_DIM)
        values = low(low_back(product('the,thed->thd', value_hot * value_gate, expert_values)))
        attended = low(low_back(attend(queries, key_rows, values)))
        output_gate = jax.nn.sigmoid(low_back(product('td,dk->tk', inputs, output_router))).reshape(seq_len, HEADS, ATT_EXPERTS)
        mixed = low((output_hot * output_gate)[..., None] * attended[:, :, None, :]).reshape(seq_len, HEADS * ATT_EXPERTS * HEAD_DIM)
        middle = inputs + low_back(product('tk,kd->td', mixed, output_weight))
        middle_low = low(middle)

        def expert_block(element):
            rows_low, hot_rows = element
            router_gate = jax.nn.sigmoid(low_back(product('td,de->te', rows_low, expert_router)))
            hidden_pre = low_back(product('td,dk->tk', rows_low, up_weight))
            gates_wide = jnp.repeat(hot_rows * router_gate, EXPERT_WIDTH, axis=1)
            hidden = low(jax.nn.silu(hidden_pre) * gates_wide)
            return low_back(product('tk,kd->td', hidden, down_weight))
        block_rows = min(1024, seq_len)
        block_total = seq_len // block_rows
        branch = lax.map(jax.checkpoint(expert_block), (middle_low.reshape(block_total, block_rows, D), expert_hot.reshape(block_total, block_rows, EXPERTS)))
        return middle + branch.reshape(seq_len, D)
    layer_out, pullback = jax.vjp(forward, tokens.astype(jnp.float32), ln_gain.astype(jnp.float32), w_query.astype(jnp.float32), w_key.astype(jnp.float32), w_value.astype(jnp.float32), w_output.astype(jnp.float32), route_value.astype(jnp.float32), route_output.astype(jnp.float32), route_expert.astype(jnp.float32), w_up.astype(jnp.float32), w_down.astype(jnp.float32))
    gradients = pullback(out_grad.astype(jnp.float32))
    return (layer_out, gradients[0], gradients[1], gradients[2], gradients[3], gradients[4], gradients[5], gradients[6], gradients[7], gradients[8], gradients[9], gradients[10])
```

```python
import functools

import jax
import jax.numpy as jnp
from jax import lax
from jax.experimental import pallas as pl
from jax.experimental.pallas import tpu as pltpu
from jax.sharding import PartitionSpec as P

ATT_BLOCK = 256
ln_eps = 1e-05
rope_base = 10000.0
MIB = 1 << 20
BF = jnp.bfloat16
F32 = jnp.float32


def swap(value, axis, mask):
    size = lax.axis_size(axis)
    return lax.ppermute(value, axis, [(i, i ^ mask) for i in range(size)])


def gather_blk(value, size=None):
    size = size or lax.axis_size("blk")
    pieces = []
    for mask in range(0, size, 2):
        mine = value if mask == 0 else swap(value, "blk", mask)
        pieces += [mine, swap(mine, "blk", 1)]
    return pieces


def reduce_blk(parts):
    size = len(parts)
    total = None
    for mask in [*range(2, size, 2), 0]:
        pair = parts[mask].astype(F32) + swap(parts[mask + 1], "blk", 1).astype(F32)
        if mask:
            pair = swap(pair.astype(BF), "blk", mask).astype(F32)
        total = pair if total is None else total + pair
    return total


def gather_head(value):
    size = lax.axis_size("head")
    return [value] + [swap(value, "head", mask) for mask in range(1, size)]


def rotate(values, cosine, sine):
    half = values.shape[-1] // 2
    first, second = values[..., :half], values[..., half:]
    return jnp.concatenate(
        [first * cosine - second * sine, second * cosine + first * sine], axis=-1
    )


def nt(left, right):
    return lax.dot_general(left, right, (((1,), (1,)), ((), ())), preferred_element_type=F32)


def tn(left, right):
    return lax.dot_general(left, right, (((0,), (0,)), ((), ())), preferred_element_type=F32)


def nn(left, right):
    return jnp.dot(left, right, preferred_element_type=F32)


def block_of(place, blk, head, tok_rows, span):
    return (blk * span + (head ^ (place // tok_rows)) * tok_rows + place % tok_rows) // ATT_BLOCK


def own_allowed(blk, head, tok_rows, span):
    keys = lax.broadcasted_iota(jnp.int32, (span, span), 0)
    queries = lax.broadcasted_iota(jnp.int32, (span, span), 1)
    return block_of(keys, blk, head, tok_rows, span) <= block_of(
        queries, blk, head, tok_rows, span
    )


def attend_kernel(groups, tok_rows, scale, at_ref, q_ref, *refs):
    kv_refs = refs[:groups]
    o_ref, lse_ref, top_ref, total_ref, acc_ref = refs[groups:]
    span, size = q_ref.shape
    blk, head = at_ref[0], at_ref[1]
    queries = q_ref[...]

    def advance(kv_ref, first):
        scores = nt(kv_ref[:, :size], queries) * scale
        if first:
            scores = jnp.where(own_allowed(blk, head, tok_rows, span), scores, -jnp.inf)
            top = jnp.max(scores, 0, keepdims=True)
        else:
            top = jnp.maximum(top_ref[...], jnp.max(scores, 0, keepdims=True))
        weights = jnp.exp(scores - top)
        mass = jnp.sum(weights, 0, keepdims=True)
        term = tn(kv_ref[:, size:], weights.astype(BF))
        if first:
            total_ref[...] = mass
            acc_ref[...] = term
        else:
            fade = jnp.exp(top_ref[...] - top)
            total_ref[...] = total_ref[...] * fade + mass
            acc_ref[...] = acc_ref[...] * fade + term
        top_ref[...] = top

    advance(kv_refs[0], True)
    for mask in range(1, groups):
        pl.when((blk ^ mask) < blk)(functools.partial(advance, kv_refs[mask], False))
    lse_ref[...] = top_ref[...] + jnp.log(total_ref[...])
    o_ref[...] = (acc_ref[...] / total_ref[...]).T.astype(BF)


def attend(at, queries, pieces, tok_rows, scale):
    span, size = queries.shape
    groups = len(pieces)
    vmem = pl.BlockSpec(memory_space=pltpu.VMEM)
    return pl.pallas_call(
        functools.partial(attend_kernel, groups, tok_rows, scale),
        out_shape=(
            jax.ShapeDtypeStruct((span, size), BF),
            jax.ShapeDtypeStruct((1, span), F32),
        ),
        in_specs=[pl.BlockSpec(memory_space=pltpu.SMEM)] + [vmem] * (1 + groups),
        out_specs=(vmem, vmem),
        scratch_shapes=[
            pltpu.VMEM((1, span), F32),
            pltpu.VMEM((1, span), F32),
            pltpu.VMEM((size, span), F32),
        ],
        compiler_params=pltpu.CompilerParams(vmem_limit_bytes=32 * MIB),
        cost_estimate=pl.CostEstimate(
            flops=4 * groups * span * span * size,
            bytes_accessed=(2 * groups + 2) * span * size * 2,
            transcendentals=groups * span * span,
        ),
        name="attend",
    )(at, queries, *pieces)


def attend_back_kernel(groups, tok_rows, scale, at_ref, *refs):
    kv_refs = refs[:groups]
    q_refs = refs[groups : 2 * groups]
    dout_refs = refs[2 * groups : 3 * groups]
    stat_refs = refs[3 * groups : 4 * groups]
    dq_ref, dk_ref, dv_ref, dq_acc = refs[4 * groups :]
    span, size = q_refs[0].shape
    blk, head = at_ref[0], at_ref[1]

    def terms(kv_ref, q_ref, dout_ref, stat_ref, own):
        scores = nt(kv_ref[:, :size], q_ref[...]) * scale
        if own:
            scores = jnp.where(own_allowed(blk, head, tok_rows, span), scores, -jnp.inf)
        prob = jnp.exp(scores - stat_ref[0:1, :])
        prob_grad = nt(kv_ref[:, size:], dout_ref[...])
        score_grad = prob * (prob_grad - stat_ref[1:2, :]) * scale
        return prob.astype(BF), score_grad.astype(BF)

    prob, grad = terms(kv_refs[0], q_refs[0], dout_refs[0], stat_refs[0], True)
    dq_acc[...] = tn(kv_refs[0][:, :size], grad)
    dk_ref[...] = nn(grad, q_refs[0][...])
    dv_ref[...] = nn(prob, dout_refs[0][...])

    def earlier(mask):
        prob, grad = terms(kv_refs[mask], q_refs[0], dout_refs[0], stat_refs[0], False)
        dq_acc[...] += tn(kv_refs[mask][:, :size], grad)

    def later(mask):
        prob, grad = terms(kv_refs[0], q_refs[mask], dout_refs[mask], stat_refs[mask], False)
        dk_ref[...] += nn(grad, q_refs[mask][...])
        dv_ref[...] += nn(prob, dout_refs[mask][...])

    for mask in range(1, groups):
        pl.when((blk ^ mask) < blk)(functools.partial(earlier, mask))
        pl.when((blk ^ mask) > blk)(functools.partial(later, mask))
    dq_ref[...] = dq_acc[...].T


def attend_back(at, kv, queries, douts, stats, tok_rows, scale):
    span, size = queries[0].shape
    groups = len(kv)
    vmem = pl.BlockSpec(memory_space=pltpu.VMEM)
    shape = jax.ShapeDtypeStruct((span, size), F32)
    return pl.pallas_call(
        functools.partial(attend_back_kernel, groups, tok_rows, scale),
        out_shape=(shape, shape, shape),
        in_specs=[pl.BlockSpec(memory_space=pltpu.SMEM)] + [vmem] * (4 * groups),
        out_specs=(vmem, vmem, vmem),
        scratch_shapes=[pltpu.VMEM((size, span), F32)],
        compiler_params=pltpu.CompilerParams(vmem_limit_bytes=40 * MIB),
        cost_estimate=pl.CostEstimate(
            flops=8 * groups * span * span * size,
            bytes_accessed=(4 * groups + 6) * span * size * 2,
            transcendentals=groups * span * span,
        ),
        name="attend_back",
    )(at, *kv, *queries, *douts, *stats)


def experts_kernel(
    experts,
    x_ref,
    g_ref,
    hot_ref,
    up_ref,
    down_ref,
    route_ref,
    out_ref,
    dx_ref,
    hidden_ref,
    da_ref,
    dsm_ref,
):
    rows = x_ref.shape[0]
    units = up_ref.shape[1]
    width = units // experts
    step = min(units, 256)
    x, g = x_ref[...], g_ref[...]
    gate = jax.nn.sigmoid(nn(x, route_ref[...]))
    hot = hot_ref[...]
    named = hot * gate
    dgate = jnp.zeros((rows, experts), F32)
    lane = lax.broadcasted_iota(jnp.int32, (rows, experts), 1)
    for at in range(0, units, step):
        pre_all = nn(x, up_ref[:, at : at + step])
        dh_all = nt(g, down_ref[at : at + step, :])
        for inner in range(0, step, width):
            pre, dh = pre_all[:, inner : inner + width], dh_all[:, inner : inner + width]
            expert = (at + inner) // width
            scale = named[:, expert : expert + 1]
            sig = jax.nn.sigmoid(pre)
            act = pre * sig
            slope = sig * (1.0 + pre * (1.0 - sig))
            hidden_ref[:, at + inner : at + inner + width] = (act * scale).astype(BF)
            da_ref[:, at + inner : at + inner + width] = (dh * scale * slope).astype(BF)
            dgate = jnp.where(lane == expert, jnp.sum(dh * act, -1, keepdims=True), dgate)
    dsm = (dgate * hot * gate * (1.0 - gate)).astype(BF)
    dsm_ref[...] = dsm
    out_ref[...] = nn(hidden_ref[...], down_ref[...]).astype(BF)
    dx_ref[...] = (nt(da_ref[...], up_ref[...]) + nt(dsm, route_ref[...])).astype(BF)


def run_experts(x, g, hot, up, down, route):
    rows, width = x.shape
    units = up.shape[1]
    experts = hot.shape[1]
    tile = 256

    def moving(columns):
        return pl.BlockSpec((tile, columns), lambda i: (i, 0))

    def fixed(array):
        return pl.BlockSpec(array.shape, lambda i: (0, 0))

    return pl.pallas_call(
        functools.partial(experts_kernel, experts),
        grid=(rows // tile,),
        out_shape=(
            jax.ShapeDtypeStruct((rows, width), BF),
            jax.ShapeDtypeStruct((rows, width), BF),
            jax.ShapeDtypeStruct((rows, units), BF),
            jax.ShapeDtypeStruct((rows, units), BF),
            jax.ShapeDtypeStruct((rows, experts), BF),
        ),
        in_specs=[moving(width), moving(width), moving(experts), fixed(up), fixed(down), fixed(route)],
        out_specs=(moving(width), moving(width), moving(units), moving(units), moving(experts)),
        compiler_params=pltpu.CompilerParams(vmem_limit_bytes=40 * MIB),
        cost_estimate=pl.CostEstimate(
            flops=8 * rows * width * units,
            bytes_accessed=2 * (4 * rows * width + 2 * rows * units + 2 * width * units),
            transcendentals=rows * units,
        ),
        name="experts",
    )(x, g, hot, up, down, route)


def expert_grads_kernel(groups, *refs):
    x_refs, g_refs, hidden_refs, da_refs, dsm_refs = (
        refs[i * groups : (i + 1) * groups] for i in range(5)
    )
    up_ref, down_ref, route_ref, wide, narrow, small, sems = refs[5 * groups :]

    def copies(mask):
        slot = mask % 2
        places = (
            (x_refs, wide.at[slot, 0]),
            (g_refs, wide.at[slot, 1]),
            (hidden_refs, narrow.at[slot, 0]),
            (da_refs, narrow.at[slot, 1]),
            (dsm_refs, small.at[slot]),
        )
        return [
            pltpu.make_async_copy(sources[mask], place, sems.at[slot, i])
            for i, (sources, place) in enumerate(places)
        ]

    for move in copies(0):
        move.start()
    for mask in range(groups):
        slot = mask % 2
        if mask + 1 < groups:
            for move in copies(mask + 1):
                move.start()
        for move in copies(mask):
            move.wait()
        up = tn(wide[slot, 0], narrow[slot, 1])
        down = tn(narrow[slot, 0], wide[slot, 1])
        route = tn(wide[slot, 0], small[slot])
        if mask == 0:
            up_ref[...], down_ref[...], route_ref[...] = up, down, route
        else:
            up_ref[...] += up
            down_ref[...] += down
            route_ref[...] += route


def expert_grads(rows, grads, hidden, das, dsms):
    groups = len(rows)
    span, width = rows[0].shape
    units, experts = das[0].shape[1], dsms[0].shape[1]
    any_spec = pl.BlockSpec(memory_space=pl.ANY)
    vmem = pl.BlockSpec(memory_space=pltpu.VMEM)
    return pl.pallas_call(
        functools.partial(expert_grads_kernel, groups),
        out_shape=(
            jax.ShapeDtypeStruct((width, units), F32),
            jax.ShapeDtypeStruct((units, width), F32),
            jax.ShapeDtypeStruct((width, experts), F32),
        ),
        in_specs=[any_spec] * (5 * groups),
        out_specs=(vmem, vmem, vmem),
        scratch_shapes=[
            pltpu.VMEM((2, 2, span, width), BF),
            pltpu.VMEM((2, 2, span, units), BF),
            pltpu.VMEM((2, span, experts), BF),
            pltpu.SemaphoreType.DMA((2, 5)),
        ],
        compiler_params=pltpu.CompilerParams(vmem_limit_bytes=48 * MIB),
        cost_estimate=pl.CostEstimate(
            flops=4 * groups * span * width * units,
            bytes_accessed=4 * groups * span * (width + units) + 8 * width * units,
            transcendentals=0,
        ),
        name="expert_grads",
    )(*rows, *grads, *hidden, *das, *dsms)


def on_device(
    tokens,
    out_grad,
    ln_gain,
    w_query,
    w_key,
    w_value,
    w_output,
    route_value,
    route_output,
    route_expert,
    w_up,
    w_down,
    value_ids,
    output_ids,
    expert_ids,
):
    groups, heads = lax.axis_size("blk"), lax.axis_size("head")
    blk, head = lax.axis_index("blk"), lax.axis_index("head")
    tok_rows, width = tokens.shape
    head_count = value_ids.shape[1]
    att_count = route_value.shape[1] // head_count
    head_size = w_query.shape[1] // head_count
    experts = route_expert.shape[1]
    span = tok_rows * heads
    own_rows = w_query.shape[0]
    mixed = att_count * head_size
    scale = head_size ** (-0.5)
    device = blk * heads + head
    at = jnp.stack([blk, head]).astype(jnp.int32)

    used = 2 * head_size + mixed + att_count + head_count * att_count + 1
    packed_width = -(-used // 128) * 128
    per_head = []
    for h in range(head_count):
        per_head.append(
            jnp.concatenate(
                [
                    w_query[:, h * head_size : (h + 1) * head_size],
                    w_key[:, h * head_size : (h + 1) * head_size],
                    w_value[:, h * mixed : (h + 1) * mixed],
                    route_value[:, h * att_count : (h + 1) * att_count],
                    route_output,
                    ln_gain[:, None],
                    jnp.zeros((own_rows, packed_width - used), BF),
                ],
                axis=1,
            )
        )
    by_head = lax.all_to_all(jnp.stack(per_head), "head", 0, 0, tiled=True)
    by_head = by_head.reshape(heads * own_rows, packed_width)
    order = blk ^ jnp.arange(groups)
    weights = jnp.stack(gather_blk(by_head))[order].reshape(width, packed_width)

    wide = jnp.concatenate(gather_head(tokens))
    ids_all = jnp.concatenate(
        [value_ids.reshape(tok_rows, -1), output_ids.reshape(tok_rows, -1)], axis=1
    ).T
    ids_group = jnp.concatenate(gather_head(ids_all), axis=1).T
    value_hot = jnp.sum(
        (
            ids_group[:, : 2 * head_count].reshape(span, head_count, 2)[..., None]
            == jnp.arange(att_count)
        ).astype(F32),
        2,
    )
    output_hot = jnp.sum(
        (
            ids_group[:, 2 * head_count :].reshape(span, head_count, 2)[..., None]
            == jnp.arange(att_count)
        ).astype(F32),
        2,
    )
    output_full = lax.all_gather(w_output, ("blk", "head"), axis=0, tiled=True)

    places = jnp.arange(span)
    places = blk * span + (head ^ (places // tok_rows)) * tok_rows + places % tok_rows
    half = head_size // 2
    frequency = rope_base ** (-jnp.arange(half, dtype=F32) / half)
    angles = places.astype(F32)[:, None] * frequency[None, :]
    cosine, sine = jnp.cos(angles), jnp.sin(angles)

    inputs = wide.astype(F32)
    centre = jnp.mean(inputs, -1, keepdims=True)
    shifted = inputs - centre
    inv_std = lax.rsqrt(jnp.mean(shifted * shifted, -1, keepdims=True) + ln_eps)
    normal = shifted * inv_std
    gain = weights[:, used - 1].astype(F32)
    normed = (normal * gain).astype(BF)
    qk_weight = weights[:, : 2 * head_size]
    v_weight = weights[:, 2 * head_size :]
    qk_pre = nn(normed, qk_weight)
    from_tokens = nn(wide, v_weight)
    query = rotate(qk_pre[:, :head_size], cosine, sine).astype(BF)
    key = rotate(qk_pre[:, head_size:], cosine, sine).astype(BF)
    value_gate = jax.nn.sigmoid(from_tokens[:, mixed : mixed + att_count])
    my_value_hot = lax.dynamic_index_in_dim(value_hot, head, 1, keepdims=False)
    value_weight = my_value_hot * value_gate
    expert_values = from_tokens[:, :mixed].reshape(span, att_count, head_size)
    value = jnp.sum(value_weight[..., None] * expert_values, 1).astype(BF)
    output_gate = jax.nn.sigmoid(
        from_tokens[:, mixed + att_count : mixed + att_count + head_count * att_count]
    ).reshape(span, head_count, att_count)
    output_weight = output_hot * output_gate

    kv = gather_blk(jnp.concatenate([key, value], axis=1))
    mine, log_total = attend(at, query, kv, tok_rows, scale)

    def reorder(piece, mask):
        return jnp.concatenate(
            [piece[(s ^ mask) * tok_rows : ((s ^ mask) + 1) * tok_rows] for s in range(heads)]
        )

    got = [reorder(piece, mask) for mask, piece in enumerate(gather_head(mine))]
    head_order = head ^ jnp.arange(heads)
    head_out = jnp.stack(got)[head_order]
    weight_by_head = output_weight.transpose(1, 0, 2)
    mixed_heads = (weight_by_head[..., None] * head_out[:, :, None, :].astype(F32)).astype(BF)
    mixed_flat = mixed_heads.transpose(1, 0, 2, 3).reshape(span, head_count * mixed)
    middle = inputs + nn(mixed_flat, output_full)
    middle_low = middle.astype(BF)

    grad_group = jnp.concatenate(gather_head(out_grad))
    ids_expert = jnp.concatenate(gather_head(expert_ids.T), axis=1)
    first = device * experts + jnp.arange(experts)
    branch = group_grad = weight_grads = None
    near = min(groups, 8)
    for far in range(0, groups, near):
        base = (middle_low, grad_group, ids_expert)
        if far:
            base, branch, group_grad, weight_grads = lax.optimization_barrier(
                (base, branch, group_grad, weight_grads)
            )
            base = [swap(value, "blk", far) for value in base]
        rows, grads, ids_pieces = (gather_blk(value, near) for value in base)
        hots = [
            jnp.any(ids[:, :, None] == first, axis=0).astype(F32) for ids in ids_pieces
        ]
        done = [
            run_experts(x, g, hot, w_up, w_down, route_expert)
            for x, g, hot in zip(rows, grads, hots)
        ]
        outs, dxs, hidden, das, dsms = zip(*done)
        terms = expert_grads(rows, grads, hidden, das, dsms)
        dx_sum = reduce_blk(dxs)
        out_sum = reduce_blk(outs)
        if far:
            branch = branch + swap(out_sum.astype(BF), "blk", far).astype(F32)
            group_grad = group_grad + swap(dx_sum.astype(BF), "blk", far).astype(F32)
            weight_grads = [old + new for old, new in zip(weight_grads, terms)]
        else:
            branch, group_grad, weight_grads = out_sum, dx_sum, terms
    grad_up, grad_down, grad_route_expert = weight_grads

    group_grad = group_grad + jnp.concatenate(
        [out_grad.astype(F32), jnp.zeros((span - tok_rows, width), F32)]
    )
    group_low = group_grad.astype(BF)
    du = nt(group_low, output_full).reshape(span, head_count, att_count, head_size)
    dout_part = jnp.einsum("thed,the->htd", du, output_weight)
    dso_part = jnp.einsum("thed,htd->het", du, head_out.astype(F32))
    pad = -att_count % 8
    dso_part = jnp.concatenate([dso_part, jnp.zeros((head_count, pad, span), F32)], axis=1)
    dout = lax.dynamic_index_in_dim(dout_part, head, 0, keepdims=False)
    dso = lax.dynamic_index_in_dim(dso_part, head, 0, keepdims=False)
    for mask in range(1, heads):
        there = head ^ mask
        part = lax.dynamic_index_in_dim(dout_part, there, 0, keepdims=False).astype(BF)
        dout = dout + reorder(swap(part, "head", mask), mask).astype(F32)
        small = swap(lax.dynamic_index_in_dim(dso_part, there, 0, keepdims=False), "head", mask)
        dso = dso + reorder(small.T, mask).T
    dout_low = dout.astype(BF)
    my_gate = lax.dynamic_index_in_dim(output_gate, head, 1, keepdims=False)
    my_hot = lax.dynamic_index_in_dim(output_hot, head, 1, keepdims=False)
    output_lgrad = (dso.T[:, :att_count] * my_hot * my_gate * (1.0 - my_gate)).astype(BF)

    delta = jnp.sum(dout_low.astype(F32) * mine.astype(F32), -1)
    stats = jnp.concatenate([log_total, delta[None, :], jnp.zeros((6, span), F32)])
    douts = gather_blk(dout_low)
    stat_pieces = gather_blk(stats)
    queries = gather_blk(query)
    dq, dk, dv = attend_back(at, kv, queries, douts, stat_pieces, tok_rows, scale)

    flat_grad = tn(mixed_flat, group_low).astype(BF)
    out_rows = w_output.shape[0]
    by_group = flat_grad.reshape(groups, heads * out_rows, width)
    mine_rows = reduce_blk(
        [lax.dynamic_index_in_dim(by_group, blk ^ m, 0, keepdims=False) for m in range(groups)]
    ).reshape(heads, out_rows, width)
    grad_output = lax.dynamic_index_in_dim(mine_rows, head, 0, keepdims=False)
    for mask in range(1, heads):
        part = lax.dynamic_index_in_dim(mine_rows, head ^ mask, 0, keepdims=False).astype(BF)
        grad_output = grad_output + swap(part, "head", mask).astype(F32)

    query_back = rotate(dq, cosine, -sine).astype(BF)
    key_back = rotate(dk, cosine, -sine).astype(BF)
    value_back = dv.astype(BF).astype(F32)
    qk_back = jnp.concatenate([query_back, key_back], axis=1)
    dexpert = (value_weight[..., None] * value_back[:, None, :]).astype(BF).reshape(span, mixed)
    dvweight = jnp.sum(value_back[:, None, :] * expert_values, -1)
    value_lgrad = (dvweight * my_value_hot * value_gate * (1.0 - value_gate)).astype(BF)
    spread = jnp.where(
        (jnp.arange(head_count) == head)[None, :, None], output_lgrad[:, None, :], 0
    ).astype(BF)
    tail = packed_width - used + 1
    v_back = jnp.concatenate(
        [
            dexpert,
            value_lgrad,
            spread.reshape(span, head_count * att_count),
            jnp.zeros((span, tail), BF),
        ],
        axis=1,
    )
    grad_normed = nt(qk_back, qk_weight)
    grad_gain = jnp.sum(grad_normed * normal, 0)
    grad_normal = grad_normed * gain
    part = (
        group_grad
        + nt(v_back, v_weight)
        + inv_std
        * (
            grad_normal
            - jnp.mean(grad_normal, -1, keepdims=True)
            - normal * jnp.mean(grad_normal * normal, -1, keepdims=True)
        )
    )
    grad_input = part[:tok_rows]
    for mask in range(1, heads):
        piece = part[mask * tok_rows : (mask + 1) * tok_rows].astype(BF)
        grad_input = grad_input + swap(piece, "head", mask).astype(F32)

    grad_tok = tn(wide, v_back)
    lane = jnp.arange(grad_tok.shape[1])
    grad_tok = jnp.where(lane[None, :] == used - 1 - 2 * head_size, grad_gain[:, None], grad_tok)
    packed = jnp.concatenate([tn(normed, qk_back), grad_tok], axis=1).astype(BF)
    packed = packed.reshape(groups, heads * own_rows, packed_width)
    summed = reduce_blk(
        [lax.dynamic_index_in_dim(packed, blk ^ m, 0, keepdims=False) for m in range(groups)]
    )
    summed = lax.all_to_all(
        summed.astype(BF).reshape(heads, own_rows, packed_width), "head", 0, 0, tiled=True
    ).astype(F32)

    def columns(first, count):
        return summed[:, :, first : first + count].transpose(1, 0, 2).reshape(own_rows, -1)

    grad_query = columns(0, head_size)
    grad_key = columns(head_size, head_size)
    grad_value = columns(2 * head_size, mixed)
    grad_value_router = columns(2 * head_size + mixed, att_count)
    routed = summed[:, :, 2 * head_size + mixed + att_count : used]
    grad_output_router = jnp.sum(routed[:, :, :-1], 0)
    grad_gain_out = jnp.sum(routed[:, :, -1], 0)

    layer_out = middle[:tok_rows] + branch[:tok_rows]
    for mask in range(1, heads):
        piece = branch[mask * tok_rows : (mask + 1) * tok_rows].astype(BF)
        layer_out = layer_out + swap(piece, "head", mask).astype(F32)

    return (
        layer_out,
        grad_input,
        grad_gain_out,
        grad_query,
        grad_key,
        grad_value,
        grad_output,
        grad_value_router,
        grad_output_router,
        grad_route_expert,
        grad_up,
        grad_down,
    )


def solution(mesh):
    both = P(("blk", "head"), None)
    columns = P(None, ("blk", "head"))
    vector = P(("blk", "head"))
    return jax.shard_map(
        on_device,
        mesh=mesh,
        in_specs=(
            both, both, vector, both, both, both, both, both, both, columns, columns, both,
            P(("blk", "head"), None, None), P(("blk", "head"), None, None), both,
        ),
        out_specs=(
            both, both, vector, both, both, both, both, both, both, columns, columns, both,
        ),
        check_vma=False,
    )
```

```python
import functools

import jax
import jax.numpy as jnp
from jax import lax
from jax.experimental import pallas as pl
from jax.experimental.pallas import tpu as pltpu
from jax.sharding import PartitionSpec as P

ATT_BLOCK = 256
ln_eps = 1e-05
rope_base = 10000.0
MIB = 1 << 20
LANES = 128
TILE = 256
BF = jnp.bfloat16
F32 = jnp.float32
VMEM = pl.BlockSpec(memory_space=pltpu.VMEM)
SMEM = pl.BlockSpec(memory_space=pltpu.SMEM)
ANY = pl.BlockSpec(memory_space=pl.ANY)
CHEAP = pl.CostEstimate(flops=0, bytes_accessed=0, transcendentals=0)
PARAMS = pltpu.CompilerParams(vmem_limit_bytes=56 * MIB)


def swap(value, axis, mask):
    size = lax.axis_size(axis)
    return lax.ppermute(value, axis, [(i, i ^ mask) for i in range(size)])


def gather_blk(value):
    far = [value] + [swap(value, "blk", m) for m in range(2, lax.axis_size("blk"), 2)]
    pieces = []
    for mine in far:
        pieces += [mine, swap(mine, "blk", 1)]
    return pieces


def gather_head(value):
    return [value] + [swap(value, "head", m) for m in range(1, lax.axis_size("head"))]


def hold_kernel(*refs):
    del refs


def hold(value, *tokens):
    return pl.pallas_call(
        hold_kernel,
        out_shape=jax.ShapeDtypeStruct(value.shape, value.dtype),
        in_specs=[ANY] * (1 + len(tokens)),
        out_specs=ANY,
        input_output_aliases={0: 0},
        cost_estimate=CHEAP,
        name="hold",
    )(value, *tokens)


def add_low(left, right):
    return (left.astype(F32) + right.astype(F32)).astype(BF)


def shape(dims, dtype):
    return jax.ShapeDtypeStruct(dims, dtype)


def nt(left, right):
    return lax.dot_general(left, right, (((1,), (1,)), ((), ())), preferred_element_type=F32)


def tn(left, right):
    return lax.dot_general(left, right, (((0,), (0,)), ((), ())), preferred_element_type=F32)


def nn(left, right):
    return jnp.dot(left, right, preferred_element_type=F32)


def turn(values, cosine, sine):
    return values * cosine + pltpu.roll(values, values.shape[-1] // 2, 1) * sine


def block_of(place, blk, head, tok_rows, span):
    return (blk * span + (head ^ (place // tok_rows)) * tok_rows + place % tok_rows) // ATT_BLOCK


def own_allowed(blk, head, tok_rows, span):
    keys = lax.broadcasted_iota(jnp.int32, (span, span), 0)
    queries = lax.broadcasted_iota(jnp.int32, (span, span), 1)
    return block_of(keys, blk, head, tok_rows, span) <= block_of(
        queries, blk, head, tok_rows, span
    )


def norm_of(values):
    centre = jnp.mean(values, -1, keepdims=True)
    shifted = values - centre
    inv_std = lax.rsqrt(jnp.mean(shifted * shifted, -1, keepdims=True) + ln_eps)
    return shifted * inv_std, inv_std


def high_low(values):
    high = values.astype(BF)
    return high, (values - high.astype(F32)).astype(BF)


def gain_row(weights_ref, lane, first):
    rows = weights_ref.shape[0]
    parts = []
    for at in range(0, rows, LANES):
        block = weights_ref[at : at + LANES, first : first + LANES].astype(F32)
        parts.append(block.T[lane : lane + 1])
    return jnp.concatenate(parts, axis=1)


def select(rows_of_lane, valid, from_row):
    return (valid & (from_row == rows_of_lane)).astype(BF)


def pack_kernel(layout, q_ref, k_ref, v_ref, small_ref, ids_ref, out_ref):
    size, mixed, att, head_count, gain_lane = layout
    row = lax.broadcasted_iota(jnp.int32, (LANES, LANES), 0)
    lane = lax.broadcasted_iota(jnp.int32, (LANES, LANES), 1)
    small = small_ref[...]
    rows = small.shape[0]
    packed = 2 * size + mixed + LANES
    for h in range(head_count):
        out_ref[h, :rows, :size] = q_ref[:, h * size : (h + 1) * size]
        out_ref[h, :rows, size : 2 * size] = k_ref[:, h * size : (h + 1) * size]
        out_ref[h, :rows, 2 * size : 2 * size + mixed] = v_ref[:, h * mixed : (h + 1) * mixed]
        out_ref[h, : ids_ref.shape[0], packed:] = ids_ref[...].astype(BF)
        part = lane // att - 1
        source = att * head_count + att * (h ^ part) + lane % att
        source = jnp.where(lane < att, att * h + lane, source)
        source = jnp.where(lane == gain_lane, 2 * att * head_count, source)
        tail = nn(small, select(source, lane <= gain_lane, row))
        out_ref[h, :rows, 2 * size + mixed : packed] = tail.astype(BF)


def project_kernel(layout, heads, groups, named, at_ref, cos_ref, sin_ref, ids_ref, *refs):
    tok_refs, w_refs = refs[:heads], refs[heads : heads + groups]
    qkv_ref, values_ref, gate_ref, weight_ref, all_ref, normed_ref = refs[heads + groups :]
    size, mixed, att, head_count, gain_lane = layout
    blk, head = at_ref[0], at_ref[1]
    rows = w_refs[0].shape[0]
    tok_rows = tok_refs[0].shape[0]
    width = normed_ref.shape[1]
    span = normed_ref.shape[0]
    for mask in range(groups):
        start = pl.multiple_of((blk ^ mask) * rows, rows)
        all_ref[pl.ds(start, rows), :] = w_refs[mask][...]
    gain = gain_row(all_ref, gain_lane, 2 * size + mixed)
    for s in range(heads):
        normal, _ = norm_of(tok_refs[s][...].astype(F32))
        normed_ref[s * tok_rows : (s + 1) * tok_rows, :] = (normal * gain).astype(BF)
    pre = nn(normed_ref[...], all_ref[:, : 2 * size])
    cosine, sine = cos_ref[...], sin_ref[...]
    qkv_ref[:, :size] = turn(pre[:, :size], cosine, sine).astype(BF)
    qkv_ref[:, size : 2 * size] = turn(pre[:, size:], cosine, sine).astype(BF)
    wide = jnp.concatenate([ref[...] for ref in tok_refs])
    marks = []
    for s in range(heads):
        ids = ids_ref[head ^ s].astype(F32)
        ids = jnp.concatenate([ids, jnp.zeros((LANES - ids.shape[0], tok_rows), F32)])
        marks.append(ids.T.astype(BF))
    marks = jnp.concatenate(marks)
    row = lax.broadcasted_iota(jnp.int32, (LANES, LANES), 0)
    lane = lax.broadcasted_iota(jnp.int32, (LANES, LANES), 1)
    column = named * head_count + named * (head ^ (lane // att - 1))
    column = jnp.where(lane < att, named * head, column)
    valid = lane < att * (head_count + 1)
    expert = lax.broadcasted_iota(jnp.int32, (span, LANES), 1)
    inside = expert < att * (head_count + 1)
    expert = (expert % att).astype(F32)
    hot = jnp.zeros((span, LANES), F32)
    for k in range(named):
        ids = nn(marks, select(column + k, valid, row))
        hot = jnp.where(inside & (ids == expert), 1.0, hot)
    gates = jax.nn.sigmoid(nn(wide, all_ref[:, 2 * size + mixed :]))
    weight = hot * gates
    gate_ref[...] = gates
    weight_ref[...] = weight
    value = jnp.zeros((span, size), F32)
    first = 2 * size
    expert_values = nn(wide, all_ref[:, first : first + mixed])
    values_ref[...] = expert_values
    for e in range(att):
        value += weight[:, e : e + 1] * expert_values[:, e * size : (e + 1) * size]
    qkv_ref[:, 2 * size :] = value.astype(BF)


def attend_kernel(groups, tok_rows, scale, at_ref, *refs):
    refs, (o_ref, lse_ref, top_ref, total_ref, acc_ref) = refs[:groups], refs[-5:]
    span = refs[0].shape[0]
    size = refs[0].shape[1] // 3
    blk, head = at_ref[0], at_ref[1]
    queries = refs[0][:, :size]

    def advance(ref, first):
        scores = nt(ref[:, size : 2 * size], queries) * scale
        if first:
            scores = jnp.where(own_allowed(blk, head, tok_rows, span), scores, -jnp.inf)
            top = jnp.max(scores, 0, keepdims=True)
        else:
            top = jnp.maximum(top_ref[...], jnp.max(scores, 0, keepdims=True))
        weights = jnp.exp(scores - top)
        mass = jnp.sum(weights, 0, keepdims=True)
        term = tn(ref[:, 2 * size :], weights.astype(BF))
        if first:
            total_ref[...] = mass
            acc_ref[...] = term
        else:
            fade = jnp.exp(top_ref[...] - top)
            total_ref[...] = total_ref[...] * fade + mass
            acc_ref[...] = acc_ref[...] * fade + term
        top_ref[...] = top

    advance(refs[0], True)
    for mask in range(1, groups):
        pl.when((blk ^ mask) < blk)(functools.partial(advance, refs[mask], False))
    lse_ref[...] = top_ref[...] + jnp.log(total_ref[...])
    o_ref[...] = (acc_ref[...] / total_ref[...]).T.astype(BF)


def attend(at, qkv, tok_rows, scale, tokens):
    span, size = qkv[0].shape[0], qkv[0].shape[1] // 3
    groups = len(qkv)
    return pl.pallas_call(
        functools.partial(attend_kernel, groups, tok_rows, scale),
        out_shape=(shape((span, size), BF), shape((1, span), F32)),
        in_specs=[SMEM] + [VMEM] * groups + [ANY] * len(tokens),
        out_specs=(VMEM, VMEM),
        scratch_shapes=[
            pltpu.VMEM((1, span), F32),
            pltpu.VMEM((1, span), F32),
            pltpu.VMEM((size, span), F32),
        ],
        compiler_params=PARAMS,
        cost_estimate=CHEAP,
        name="attend",
    )(at, *qkv, *tokens)


def attend_back_kernel(groups, tok_rows, scale, at_ref, *refs):
    own_refs, dout_refs = refs[:groups], refs[groups : 2 * groups]
    dq_ref, dk_ref, dv_ref, dq_acc = refs[-4:]
    size = own_refs[0].shape[1] // 3
    span = own_refs[0].shape[0]
    blk, head = at_ref[0], at_ref[1]
    parts = span // LANES

    def stat(ref, which):
        first = span + 2 * parts * which
        high = ref[first : first + parts, :].astype(F32)
        low = ref[first + parts : first + 2 * parts, :].astype(F32)
        both = high + low
        return jnp.concatenate([both[i : i + 1] for i in range(parts)], axis=1)

    def terms(key_ref, query_ref, dout_ref, own):
        scores = nt(key_ref[:, size : 2 * size], query_ref[:, :size]) * scale
        if own:
            scores = jnp.where(own_allowed(blk, head, tok_rows, span), scores, -jnp.inf)
        prob = jnp.exp(scores - stat(dout_ref, 0))
        prob_grad = nt(key_ref[:, 2 * size :], dout_ref[:span, :])
        score_grad = prob * (prob_grad - stat(dout_ref, 1)) * scale
        return prob.astype(BF), score_grad.astype(BF)

    prob, grad = terms(own_refs[0], own_refs[0], dout_refs[0], True)
    dq_acc[...] = tn(own_refs[0][:, size : 2 * size], grad)
    dk_ref[...] = nn(grad, own_refs[0][:, :size])
    dv_ref[...] = nn(prob, dout_refs[0][:span, :])

    def earlier(mask):
        prob, grad = terms(own_refs[mask], own_refs[0], dout_refs[0], False)
        dq_acc[...] += tn(own_refs[mask][:, size : 2 * size], grad)

    def later(mask):
        prob, grad = terms(own_refs[0], own_refs[mask], dout_refs[mask], False)
        dk_ref[...] += nn(grad, own_refs[mask][:, :size])
        dv_ref[...] += nn(prob, dout_refs[mask][:span, :])

    for mask in range(1, groups):
        pl.when((blk ^ mask) < blk)(functools.partial(earlier, mask))
        pl.when((blk ^ mask) > blk)(functools.partial(later, mask))
    dq_ref[...] = dq_acc[...].T


def attend_back(at, qkv, douts, tok_rows, scale, tokens):
    span, size = qkv[0].shape[0], qkv[0].shape[1] // 3
    groups = len(qkv)
    return pl.pallas_call(
        functools.partial(attend_back_kernel, groups, tok_rows, scale),
        out_shape=(shape((span, size), F32),) * 3,
        in_specs=[SMEM] + [VMEM] * (2 * groups) + [ANY] * len(tokens),
        out_specs=(VMEM,) * 3,
        scratch_shapes=[pltpu.VMEM((size, span), F32)],
        compiler_params=PARAMS,
        cost_estimate=CHEAP,
        name="attend_back",
    )(at, *qkv, *douts, *tokens)


def mix_kernel(layout, heads, at_ref, *refs):
    o_refs, tok_refs = refs[:heads], refs[heads : 2 * heads]
    weight_ref, wo_ref = refs[2 * heads : 2 * heads + 2]
    x1_ref, low_ref, u_ref = refs[-3:]
    size, mixed, att, _, _ = layout
    head = at_ref[1]
    span = weight_ref.shape[0]
    tok_rows = span // heads

    @pl.when(pl.program_id(0) == 0)
    def _():
        for s in range(heads):
            start = (head ^ s) * mixed
            for r in range(heads):
                rows = slice(r * tok_rows, (r + 1) * tok_rows)
                there = slice((r ^ s) * tok_rows, ((r ^ s) + 1) * tok_rows)
                out = o_refs[s][there, :].astype(F32)
                for e in range(att):
                    lane = att + att * s + e
                    u_ref[rows, pl.ds(pl.multiple_of(start + e * size, size), size)] = (
                        weight_ref[rows, lane : lane + 1] * out
                    ).astype(BF)

    own = jnp.concatenate([ref[...] for ref in tok_refs]).astype(F32)
    x1 = own + nn(u_ref[...], wo_ref[...])
    x1_ref[...] = x1[:tok_rows]
    low_ref[...] = x1.astype(BF)


def mix(layout, at, outs, tok_pieces, weight, w_output, tokens):
    heads = len(outs)
    span = weight.shape[0]
    depth, width = w_output.shape
    step = min(width, 256)

    def whole(array):
        return pl.BlockSpec(array.shape, lambda i: (0, 0))

    def columns(rows):
        return pl.BlockSpec((rows, step), lambda i: (0, i))

    return pl.pallas_call(
        functools.partial(mix_kernel, layout, heads),
        grid=(width // step,),
        out_shape=(
            shape((span // heads, width), F32),
            shape((span, width), BF),
            shape((span, depth), BF),
        ),
        in_specs=[SMEM]
        + [whole(o) for o in outs]
        + [columns(span // heads)] * heads
        + [whole(weight), columns(depth)]
        + [ANY] * len(tokens),
        out_specs=(
            columns(span // heads),
            columns(span),
            pl.BlockSpec((span, depth), lambda i: (0, 0)),
        ),
        compiler_params=PARAMS,
        cost_estimate=CHEAP,
        name="mix",
    )(at, *outs, *tok_pieces, weight, w_output, *tokens)


SLOTS = 16


def experts_kernel(plan, heads, experts, top, at_ref, *refs):
    chosen, far, count, tokens = plan
    x_refs = refs[:count]
    g_hbm, up_hbm, down_hbm, route_ref = refs[count : count + 4]
    groups = len(chosen)
    outs = refs[count + 4 + tokens :]
    out_refs, dx_refs = outs[:groups], outs[groups : 2 * groups]
    xs_hbm, gs_hbm, hidden_ref, da_ref = outs[2 * groups : 2 * groups + 4]
    xbuf, gbuf, xslot, gslot, dslot, up_ref, down_ref, back, in_sem, out_sem = outs[
        2 * groups + 4 :
    ]
    oslot = xbuf
    tok_rows = gbuf.shape[2] - top
    span, width = heads * tok_rows, xbuf.shape[2]
    tall = tok_rows + top
    unit = up_ref.shape[1] // experts
    arrivals = []
    sem = 0
    for p in range(groups):
        moves = []
        row = 0
        for index in chosen[p]:
            size = x_refs[index].shape[0]
            place = xbuf.at[p, pl.ds(row, size)]
            moves.append(pltpu.make_async_copy(x_refs[index], place, in_sem.at[sem]))
            row += size
            sem += 1
        for s in range(heads):
            device = (at_ref[0] ^ (far + p)) * heads + (at_ref[1] ^ s)
            source = g_hbm.at[pl.ds(pl.multiple_of(device * tall, 16), tall)]
            moves.append(pltpu.make_async_copy(source, gbuf.at[p, s], in_sem.at[sem]))
            sem += 1
        arrivals.append(moves)
    weights = [
        pltpu.make_async_copy(up_hbm, up_ref, in_sem.at[sem]),
        pltpu.make_async_copy(down_hbm, down_ref, in_sem.at[sem + 1]),
    ]
    for moves in [*arrivals, weights]:
        for move in moves:
            move.start()

    earlier = lax.broadcasted_iota(jnp.int32, (tok_rows, tok_rows), 0)
    later = lax.broadcasted_iota(jnp.int32, (tok_rows, tok_rows), 1)
    before = (earlier < later).astype(BF)
    place = lax.broadcasted_iota(jnp.int32, (experts, SLOTS, tok_rows), 1).astype(F32)
    for p in range(groups):
        for move in arrivals[p]:
            move.wait()
        for s in range(heads):
            rows = slice(s * tok_rows, (s + 1) * tok_rows)
            ids = gbuf[p, s, tok_rows:, :tok_rows].astype(F32)
            hots = []
            for e in range(experts):
                met = ids == (at_ref[2] + e).astype(F32)
                hots.append(jnp.max(met.astype(F32), 0, keepdims=True))
            hot = jnp.concatenate(hots)
            rank = nn(hot.astype(BF), before)
            rank = jnp.where(hot > 0.0, rank, -1.0)
            here = (rank[:, None, :] == place).astype(F32).reshape(experts * SLOTS, tok_rows)
            sub = p * heads + s
            back[sub] = here.T.astype(BF)
            here = here.astype(BF)
            at = slice(sub * SLOTS, (sub + 1) * SLOTS)
            moved = nn(here, xbuf[p, rows, :]).astype(BF)
            xslot[:experts, at, :] = moved.reshape(experts, SLOTS, width)
            moved = nn(here, gbuf[p, s, :tok_rows, :]).astype(BF)
            gslot[:experts, at, :] = moved.reshape(experts, SLOTS, width)
    saves = [
        pltpu.make_async_copy(xslot.at[pl.ds(0, experts)], xs_hbm, out_sem.at[2 * groups]),
        pltpu.make_async_copy(gslot.at[pl.ds(0, experts)], gs_hbm, out_sem.at[2 * groups + 1]),
    ]
    for move in [*saves]:
        move.start()
    for move in weights:
        move.wait()

    route = route_ref[...]
    held = xslot.shape[1]
    lane = lax.broadcasted_iota(jnp.int32, (held, LANES), 1)
    for e in range(experts):
        cols = slice(e * unit, (e + 1) * unit)
        x, g = xslot[e], gslot[e]
        both = jnp.concatenate([up_ref[:, cols], route], axis=1)
        pre_all = nn(x, both)
        pre, gate = pre_all[:, :unit], jax.nn.sigmoid(pre_all[:, unit + e : unit + e + 1])
        dh = nt(g, down_ref[cols, :])
        sig = jax.nn.sigmoid(pre)
        act = pre * sig
        hidden = (act * gate).astype(BF)
        da = (dh * gate * (sig + act * (1.0 - sig))).astype(BF)
        dsm = jnp.sum(dh * act, -1, keepdims=True) * gate * (1.0 - gate)
        dsm = jnp.where(lane == e, dsm, 0.0).astype(BF)
        da = jnp.concatenate([da, dsm], axis=1)
        hidden_ref[e] = hidden
        da_ref[e] = da
        dslot[e] = nt(da, both).astype(BF)
        oslot[e] = nn(hidden, down_ref[cols, :]).astype(BF)
    for move in saves:
        move.wait()

    sends = []
    for which, slots, buf, target in ((0, dslot, gslot, dx_refs), (1, oslot, xslot, out_refs)):
        for p in range(groups):
            for s in range(heads):
                rows = slice(s * tok_rows, (s + 1) * tok_rows)
                sub = p * heads + s
                at = slice(sub * SLOTS, (sub + 1) * SLOTS)
                values = slots[:experts, at, :].reshape(experts * SLOTS, width)
                buf[p, rows, :] = nn(back[sub], values).astype(BF)
            move = pltpu.make_async_copy(buf.at[p], target[p], out_sem.at[which * groups + p])
            move.start()
            sends.append(move)
    for move in sends:
        move.wait()


def run_experts(at, far, xs, g_all, up, down, route, experts, top, heads, tokens):
    groups = len(xs)
    width, units = up.shape
    span = sum(x.shape[0] for x in xs[0])
    tok_rows = span // heads
    held = groups * heads * SLOTS
    chosen, flat = [], []
    for arrays in xs:
        chosen.append(tuple(range(len(flat), len(flat) + len(arrays))))
        flat += arrays
    plan = (chosen, far, len(flat), len(tokens))
    subs = groups * heads
    slots = pltpu.VMEM((max(experts, groups), max(held, span), width), BF)
    return pl.pallas_call(
        functools.partial(experts_kernel, plan, heads, experts, top),
        out_shape=(shape((span, width), BF),) * (2 * groups)
        + (shape((experts, held, width), BF),) * 2
        + (
            shape((experts, held, units // experts), BF),
            shape((experts, held, units // experts + LANES), BF),
        ),
        in_specs=[SMEM] + [ANY] * (len(flat) + 3) + [VMEM] + [ANY] * len(tokens),
        out_specs=(ANY,) * (2 * groups + 2) + (VMEM, VMEM),
        scratch_shapes=[
            slots,
            pltpu.VMEM((groups, heads, tok_rows + top, width), BF),
            slots,
            slots,
            pltpu.VMEM((experts, held, width), BF),
            pltpu.VMEM((width, units), BF),
            pltpu.VMEM((units, width), BF),
            pltpu.VMEM((subs, tok_rows, experts * SLOTS), BF),
            pltpu.SemaphoreType.DMA((len(flat) + subs + 2,)),
            pltpu.SemaphoreType.DMA((2 * groups + 2,)),
        ],
        compiler_params=pltpu.CompilerParams(vmem_limit_bytes=60 * MIB),
        cost_estimate=CHEAP,
        name="experts",
    )(at, *flat, g_all, up, down, route, *tokens)


def expert_grads_kernel(halves, *refs):
    x_refs, g_refs, hidden_refs, da_refs = (
        refs[i * halves : (i + 1) * halves] for i in range(4)
    )
    up_ref, down_ref, route_ref = refs[-3:]
    unit = up_ref.shape[1]
    up = down = None
    for x_ref, g_ref, hidden_ref, da_ref in zip(x_refs, g_refs, hidden_refs, da_refs):
        term = tn(x_ref[0], da_ref[0])
        up = term if up is None else up + term
        term = tn(hidden_ref[0], g_ref[0])
        down = term if down is None else down + term
    up_ref[...] = up[:, :unit]
    down_ref[...] = down

    @pl.when(pl.program_id(0) == 0)
    def _():
        route_ref[...] = up[:, unit:]

    @pl.when(pl.program_id(0) > 0)
    def _():
        route_ref[...] += up[:, unit:]


def expert_grads(results, tokens):
    halves = len(results)
    experts, held, width = results[0][0].shape
    unit = results[0][2].shape[2]

    def block(array):
        return pl.BlockSpec((1,) + array.shape[1:], lambda e: (e, 0, 0))

    flat = [result[i] for i in range(4) for result in results]
    return pl.pallas_call(
        functools.partial(expert_grads_kernel, halves),
        grid=(experts,),
        out_shape=(
            shape((width, experts * unit), F32),
            shape((experts * unit, width), F32),
            shape((width, LANES), F32),
        ),
        in_specs=[block(array) for array in flat] + [ANY] * len(tokens),
        out_specs=(
            pl.BlockSpec((width, unit), lambda e: (0, e)),
            pl.BlockSpec((unit, width), lambda e: (e, 0)),
            pl.BlockSpec((width, LANES), lambda e: (0, 0)),
        ),
        compiler_params=PARAMS,
        cost_estimate=CHEAP,
        name="expert_grads",
    )(*flat, *tokens)


def spread_kernel(layout, heads, terms, at_ref, *refs):
    term_refs = refs[:terms]
    grad_ref, wo_ref, weight_ref = refs[terms : terms + 3]
    o_refs = refs[terms + 3 : terms + 3 + heads]
    g1_ref, low_ref = refs[-2 - heads : -heads]
    send_refs = refs[-heads:]
    size, mixed, att, _, _ = layout
    head = at_ref[1]
    span = g1_ref.shape[0]
    tok_rows = span // heads
    total = term_refs[0][...].astype(F32)
    for ref in term_refs[1:]:
        total += ref[...].astype(F32)
    g1_ref[...] = total
    g1_ref[:tok_rows, :] += grad_ref[...].astype(F32)
    low_ref[...] = g1_ref[...].astype(BF)
    lane = lax.broadcasted_iota(jnp.int32, (tok_rows, LANES), 1)
    for s in range(heads):
        start = pl.multiple_of((head ^ s) * mixed, LANES)
        du = nt(low_ref[...], wo_ref[pl.ds(start, mixed), :])
        for r in range(heads):
            rows = slice(r * tok_rows, (r + 1) * tok_rows)
            there = slice((r ^ s) * tok_rows, ((r ^ s) + 1) * tok_rows)
            out = o_refs[s][there, :].astype(F32)
            dout = jnp.zeros((tok_rows, size), F32)
            dots = jnp.zeros((tok_rows, LANES), F32)
            for e in range(att):
                at = att + att * s + e
                term = du[rows, e * size : (e + 1) * size]
                dout += weight_ref[rows, at : at + 1] * term
                dots = jnp.where(lane == e, jnp.sum(term * out, -1, keepdims=True), dots)
            send_refs[s][there, :] = dout.astype(BF)
            high, low = high_low(dots.T[:8, :])
            first = span + 16 * (r ^ s)
            send_refs[s][first : first + 16, :] = jnp.concatenate([high, low])


def spread(layout, at, terms, out_grad, w_output, weight, outs, tokens):
    heads = len(outs)
    span, width = terms[0].shape
    tok_rows = span // heads
    size = outs[0].shape[1]
    return pl.pallas_call(
        functools.partial(spread_kernel, layout, heads, len(terms)),
        out_shape=(shape((span, width), F32), shape((span, width), BF))
        + (shape((span + 16 * heads, size), BF),) * heads,
        in_specs=[SMEM] + [VMEM] * (len(terms) + 3 + heads) + [ANY] * len(tokens),
        out_specs=(VMEM,) * (2 + heads),
        compiler_params=PARAMS,
        cost_estimate=CHEAP,
        name="spread",
    )(at, *terms, out_grad, w_output, weight, *outs, *tokens)


def join_kernel(heads, att, *refs):
    got_refs, (o_ref, lse_ref, gate_ref, weight_ref) = refs[:heads], refs[heads : heads + 4]
    dout_ref, dso_ref = refs[-2:]
    span, size = o_ref.shape
    tok_rows = span // heads
    parts = span // LANES
    total = got_refs[0][...].astype(F32)
    for ref in got_refs[1:]:
        total += ref[...].astype(F32)
    low = total[:span].astype(BF)
    dout_ref[:span, :] = low
    product = low.astype(F32) * o_ref[...].astype(F32)
    stats = []
    lse = lse_ref[...]
    rows = [lse[:, i * LANES : (i + 1) * LANES] for i in range(parts)]
    stats += high_low(jnp.concatenate(rows))
    rows = [
        jnp.sum(product[i * LANES : (i + 1) * LANES].T, 0, keepdims=True) for i in range(parts)
    ]
    stats += high_low(jnp.concatenate(rows))
    dout_ref[span:, :] = jnp.concatenate(stats)
    for r in range(heads):
        first = span + 16 * r
        sums = total[first : first + 8] + total[first + 8 : first + 16]
        sums = jnp.concatenate([sums, jnp.zeros((LANES - 8, LANES), F32)]).T
        rows = slice(r * tok_rows, (r + 1) * tok_rows)
        moved = pltpu.roll(sums, att, 1)
        dso_ref[rows, :] = (moved * weight_ref[rows, :] * (1.0 - gate_ref[rows, :])).astype(BF)


def join(got, mine, log_total, gate, weight, att, tokens):
    heads = len(got)
    span, size = mine.shape
    parts = span // LANES
    return pl.pallas_call(
        functools.partial(join_kernel, heads, att),
        out_shape=(shape((span + 4 * parts, size), BF), shape((span, LANES), BF)),
        in_specs=[VMEM] * (heads + 4) + [ANY] * len(tokens),
        out_specs=(VMEM, VMEM),
        compiler_params=PARAMS,
        cost_estimate=CHEAP,
        name="join",
    )(*got, mine, log_total, gate, weight, *tokens)


def output_grad_kernel(rows, groups, at_ref, u_ref, g_ref, even_ref, odd_ref, all_ref):
    all_ref[...] = tn(u_ref[...], g_ref[...]).astype(BF)
    for mask in range(groups):
        place = pl.ds(pl.multiple_of((at_ref[0] ^ mask) * rows, rows), rows)
        ref = odd_ref if mask % 2 else even_ref
        ref[mask // 2 * rows : (mask // 2 + 1) * rows, :] = all_ref[place, :]


def output_grad(at, u, g, groups):
    depth, width = u.shape[1], g.shape[1]
    half = shape((depth // 2, width), BF)
    return pl.pallas_call(
        functools.partial(output_grad_kernel, depth // groups, groups),
        out_shape=(half, half),
        in_specs=[SMEM, VMEM, VMEM],
        out_specs=(VMEM, VMEM),
        scratch_shapes=[pltpu.VMEM((depth, width), BF)],
        compiler_params=PARAMS,
        cost_estimate=CHEAP,
        name="output_grad",
    )(at, u, g)


def branch_kernel(heads, *refs):
    x1_ref, own_ref, send_refs = refs[0], refs[-heads], refs[1 - heads :]
    rows = x1_ref.shape[0]
    for s in range(heads):
        at = slice(s * rows, (s + 1) * rows)
        total = sum(ref[at, :].astype(F32) for ref in refs[1:-heads])
        if s == 0:
            own_ref[...] = x1_ref[...] + total
        else:
            send_refs[s - 1][...] = total.astype(BF)


def branch(x1, terms, heads):
    return pl.pallas_call(
        functools.partial(branch_kernel, heads),
        out_shape=(shape(x1.shape, F32),) + (shape(x1.shape, BF),) * (heads - 1),
        in_specs=[VMEM] * (1 + len(terms)),
        out_specs=(VMEM,) * heads,
        compiler_params=PARAMS,
        cost_estimate=CHEAP,
        name="branch",
    )(x1, *terms)


def finish_kernel(layout, heads, groups, at_ref, *refs):
    (
        dq_ref, dk_ref, dv_ref, cos_ref, sin_ref, values_ref, gate_ref, weight_ref, dso_ref,
        normed_ref, all_ref, g1_ref,
    ) = refs[:12]
    tok_refs = refs[12 : 12 + heads]
    part_refs = refs[-4 - heads : -4]
    even_ref, odd_ref, product_ref, all_grads = refs[-4:]
    size, mixed, att, _, gain_lane = layout
    blk = at_ref[0]
    span, width = normed_ref.shape
    tok_rows = span // heads
    cosine, sine = cos_ref[...], -sin_ref[...]
    query_back = turn(dq_ref[...], cosine, sine).astype(BF)
    key_back = turn(dk_ref[...], cosine, sine).astype(BF)
    qk_back = jnp.concatenate([query_back, key_back], axis=1)
    value_back = dv_ref[...].astype(BF).astype(F32)
    lane = lax.broadcasted_iota(jnp.int32, (span, LANES), 1)
    dots = jnp.zeros((span, LANES), F32)
    columns = []
    for e in range(att):
        columns.append((weight_ref[:, e : e + 1] * value_back).astype(BF))
        dot = jnp.sum(value_back * values_ref[:, e * size : (e + 1) * size], -1, keepdims=True)
        dots = jnp.where(lane == e, dot, dots)
    gates = gate_ref[...]
    tail = (dots * weight_ref[...] * (1.0 - gates)).astype(BF)
    tail = jnp.where(lane < att, tail, jnp.where(lane < 2 * att, dso_ref[...], jnp.zeros_like(tail)))
    v_back = jnp.concatenate(columns + [tail], axis=1)
    gain = gain_row(all_ref, gain_lane, 2 * size + mixed)
    grad_normed = nt(qk_back, all_ref[:, : 2 * size])
    grad_wide = nt(v_back, all_ref[:, 2 * size :])
    for s in range(heads):
        rows = slice(s * tok_rows, (s + 1) * tok_rows)
        normal, inv_std = norm_of(tok_refs[s][...].astype(F32))
        product_ref[rows, :] = (grad_normed[rows] * normal).astype(BF)
        grad_normal = grad_normed[rows] * gain
        part = (
            g1_ref[rows, :]
            + grad_wide[rows]
            + inv_std
            * (
                grad_normal
                - jnp.mean(grad_normal, -1, keepdims=True)
                - normal * jnp.mean(grad_normal * normal, -1, keepdims=True)
            )
        )
        part_refs[s][...] = part if s == 0 else part.astype(BF)
    own = width // groups
    gain_pick = (lane == gain_lane).astype(BF)
    wide = jnp.concatenate([ref[...] for ref in tok_refs])
    all_grads[:, : 2 * size] = tn(normed_ref[...], qk_back).astype(BF)
    from_tokens = tn(wide, v_back)
    all_grads[:, 2 * size : 2 * size + mixed] = from_tokens[:, :mixed].astype(BF)
    all_grads[:, 2 * size + mixed :] = (
        from_tokens[:, mixed:] + tn(product_ref[...], gain_pick)
    ).astype(BF)
    for mask in range(groups):
        place = pl.ds(pl.multiple_of((blk ^ mask) * own, own), own)
        ref = odd_ref if mask % 2 else even_ref
        ref[mask // 2 * own : (mask // 2 + 1) * own, :] = all_grads[place, :]


def finish(layout, heads, groups, at, tokens, *arrays):
    span, width = arrays[9].shape
    packed = arrays[10].shape[1]
    half = (width // 2, packed)
    return pl.pallas_call(
        functools.partial(finish_kernel, layout, heads, groups),
        out_shape=(shape((span // heads, width), F32),)
        + (shape((span // heads, width), BF),) * (heads - 1)
        + (shape(half, BF), shape(half, BF)),
        in_specs=[SMEM] + [VMEM] * len(arrays) + [ANY] * len(tokens),
        out_specs=(VMEM,) * (heads + 2),
        scratch_shapes=[pltpu.VMEM((span, width), BF), pltpu.VMEM((width, packed), BF)],
        compiler_params=PARAMS,
        cost_estimate=CHEAP,
        name="finish",
    )(at, *arrays, *tokens)


def on_device(
    tokens,
    out_grad,
    ln_gain,
    w_query,
    w_key,
    w_value,
    w_output,
    route_value,
    route_output,
    route_expert,
    w_up,
    w_down,
    value_ids,
    output_ids,
    expert_ids,
):
    groups, heads = lax.axis_size("blk"), lax.axis_size("head")
    blk, head = lax.axis_index("blk"), lax.axis_index("head")
    tok_rows, width = tokens.shape
    head_count, named = value_ids.shape[1:]
    att = route_value.shape[1] // head_count
    size = w_query.shape[1] // head_count
    experts = route_expert.shape[1]
    top = expert_ids.shape[1]
    span = tok_rows * heads
    own_rows = w_query.shape[0]
    mixed = att * size
    scale = size ** (-0.5)
    device = blk * heads + head
    at = jnp.stack([blk, head, device * experts]).astype(jnp.int32)
    gain_lane = att + head_count * att
    layout = (size, mixed, att, head_count, gain_lane)
    used = 2 * size + mixed + gain_lane + 1
    packed = 2 * size + mixed + LANES

    small = jnp.concatenate(
        [
            route_value,
            route_output,
            ln_gain[:, None],
            jnp.zeros((own_rows, LANES - 2 * head_count * att - 1), BF),
        ],
        axis=1,
    )
    ids_rows = 2 * named * head_count + top
    ids = jnp.concatenate(
        [
            value_ids.transpose(1, 2, 0).reshape(-1, tok_rows),
            output_ids.transpose(1, 2, 0).reshape(-1, tok_rows),
            expert_ids.T,
        ]
    )
    by_head = pl.pallas_call(
        functools.partial(pack_kernel, layout),
        out_shape=shape((head_count, max(own_rows, ids_rows), packed + tok_rows), BF),
        in_specs=[VMEM] * 5,
        out_specs=VMEM,
        compiler_params=PARAMS,
        name="pack",
    )(w_query, w_key, w_value, small, ids)
    tok_pieces = gather_head(tokens)
    by_head = lax.all_to_all(by_head, "head", 0, 0, tiled=True)
    ids_group = by_head[:, :ids_rows, packed:]
    w_pieces = gather_blk(by_head[:, :own_rows, :packed].reshape(heads * own_rows, packed))

    wo_full = lax.all_gather(w_output, ("blk", "head"), axis=0, tiled=True)

    places = jnp.arange(span)
    places = blk * span + (head ^ (places // tok_rows)) * tok_rows + places % tok_rows
    half = size // 2
    frequency = rope_base ** (-jnp.arange(half, dtype=F32) / half)
    angles = places.astype(F32)[:, None] * frequency[None, :]
    cosine, sine = jnp.cos(angles), jnp.sin(angles)
    cosine = jnp.concatenate([cosine, cosine], axis=1)
    sine = jnp.concatenate([-sine, sine], axis=1)

    qkv, expert_values, gate, weight, weights, normed = pl.pallas_call(
        functools.partial(project_kernel, layout, heads, groups, named),
        out_shape=(
            shape((span, 3 * size), BF),
            shape((span, mixed), F32),
            shape((span, LANES), F32),
            shape((span, LANES), F32),
            shape((width, packed), BF),
            shape((span, width), BF),
        ),
        in_specs=[SMEM] + [VMEM] * (3 + heads + groups),
        out_specs=(VMEM,) * 6,
        compiler_params=PARAMS,
        cost_estimate=CHEAP,
        name="project",
    )(at, cosine, sine, ids_group, *tok_pieces, *w_pieces)

    ids_row = jnp.pad(expert_ids.T.astype(BF), ((0, 0), (0, width - tok_rows)))
    g_all = lax.all_gather(
        hold(jnp.concatenate([out_grad, ids_row]), qkv), ("blk", "head"), axis=0, tiled=True
    )

    qkv_pieces = gather_blk(qkv)
    mine, log_total = attend(at, qkv_pieces, tok_rows, scale, [])
    outs = gather_head(mine)
    x1, middle, mixed_heads = mix(layout, at, outs, tok_pieces, weight, wo_full, [])

    route = jnp.pad(route_expert, ((0, 0), (0, LANES - experts)))
    near = 8
    branch_terms = grad_terms = weight_grads = None

    def pair_sum(parts, mask):
        return add_low(parts[mask], swap(parts[mask + 1], "blk", 1))

    for far in range(0, groups, near):
        base = middle
        if far:
            base, *old = lax.optimization_barrier(
                (base, branch_terms, grad_terms, *weight_grads)
            )
            branch_terms, grad_terms, *weight_grads = old
            base = swap(base, "blk", far)
        even = {0: [base], 2: [swap(base, "blk", 2)], 4: [swap(base, "blk", 4)]}
        even[6] = [
            swap(even[2][0][: span // 2], "blk", 4),
            swap(even[4][0][span // 2 :], "blk", 2),
        ]
        xs = []
        for mask in range(0, near, 2):
            xs += [even[mask], [swap(x, "blk", 1) for x in even[mask]]]
        done = run_experts(
            at, far, xs, g_all, w_up, w_down, route, experts, top, heads, []
        )
        outs_all, dxs_all = done[:near], done[near : 2 * near]
        sums = [pair_sum(dxs_all, m) for m in (2, 4, 6)]
        grad_round = [dxs_all[0], swap(dxs_all[1], "blk", 1)]
        grad_round += [swap(value, "blk", m) for m, value in zip((2, 4, 6), sums)]
        terms = expert_grads([done[2 * near :]], sums)
        out_sums = [hold(pair_sum(outs_all, m), sums[-1]) for m in (2, 4, 6)]
        branch_round = [outs_all[0], swap(outs_all[1], "blk", 1)]
        out_sums = [hold(value, grad_round[-1]) for value in out_sums]
        branch_round += [swap(value, "blk", m) for m, value in zip((2, 4), out_sums)]
        if groups > near:
            branch_round.append(swap(out_sums[2], "blk", 6))
        if groups > near:
            def whole(terms):
                return functools.reduce(lambda a, b: a + b, [t.astype(F32) for t in terms])

            out_sum, dx_sum = whole(branch_round), whole(grad_round)
            if far:
                out_sum = branch_terms + swap(out_sum.astype(BF), "blk", far).astype(F32)
                dx_sum = grad_terms + swap(dx_sum.astype(BF), "blk", far).astype(F32)
                weight_grads = [old + new for old, new in zip(weight_grads, terms)]
            else:
                weight_grads = terms
            branch_terms, grad_terms = out_sum, dx_sum
        else:
            branch_terms, grad_terms, weight_grads = branch_round, grad_round, terms
    early = [*out_sums, weight_grads[2]]
    arrived = branch_round[2:4]
    if groups > near:
        branch_terms, grad_terms = [branch_terms], [grad_terms]
    grad_up, grad_down, grad_route_expert = weight_grads
    grad_route_expert = grad_route_expert[:, :experts]

    g1, g1_low, *sends = spread(layout, at, grad_terms, out_grad, wo_full, weight, outs, early)
    even, odd = output_grad(at, mixed_heads, g1_low, groups)
    got = [sends[0]] + [swap(sends[m], "head", m) for m in range(1, heads)]
    dout, dso = join(got, mine, log_total, gate, weight, att, [odd])
    dout_pieces = gather_blk(hold(dout, *arrived))
    dq, dk, dv = attend_back(at, qkv_pieces, dout_pieces, tok_rows, scale, [])

    if groups == near:
        branch_terms = branch_terms + [swap(hold(out_sums[2], *dout_pieces), "blk", 6)]
    layer_out, *outputs = branch(x1, branch_terms, heads)

    out_rows = w_output.shape[0]
    pair_sums = add_low(even, swap(hold(odd, *dout_pieces), "blk", 1))
    pair_sums = hold(pair_sums, outputs[0]).reshape(groups // 2, heads * out_rows, width)
    rows_sum = pair_sums[0].astype(F32)
    for index in range(1, groups // 2):
        rows_sum = rows_sum + swap(pair_sums[index], "blk", 2 * index).astype(F32)
    rows_sum = rows_sum.reshape(heads, out_rows, width)
    grad_output = lax.dynamic_index_in_dim(rows_sum, head, 0, keepdims=False)
    for mask in range(1, heads):
        part = lax.dynamic_index_in_dim(rows_sum, head ^ mask, 0, keepdims=False).astype(BF)
        grad_output = grad_output + swap(part, "head", mask).astype(F32)
        layer_out = layer_out + swap(outputs[mask - 1], "head", mask).astype(F32)

    grad_input, *parts, even_rows, odd_rows = finish(
        layout, heads, groups, at, [pair_sums], dq, dk, dv, cosine, sine, expert_values, gate, weight, dso,
        normed, weights, g1, *tok_pieces,
    )
    pairs = add_low(even_rows, swap(odd_rows, "blk", 1))
    own = width // groups
    summed = pairs[:own].astype(F32)
    for index in range(1, groups // 2):
        piece = pairs[index * own : (index + 1) * own]
        summed = summed + swap(piece, "blk", 2 * index).astype(F32)
    for mask in range(1, heads):
        grad_input = grad_input + swap(parts[mask - 1], "head", mask).astype(F32)
    summed = lax.all_to_all(
        summed.astype(BF).reshape(heads, own_rows, packed), "head", 0, 0, tiled=True
    ).astype(F32)

    def columns(first, count):
        return summed[:, :, first : first + count].transpose(1, 0, 2).reshape(own_rows, -1)

    grad_query = columns(0, size)
    grad_key = columns(size, size)
    grad_value = columns(2 * size, mixed)
    grad_value_router = columns(2 * size + mixed, att)
    grad_output_router = columns(2 * size + mixed + att, att)
    grad_gain = jnp.sum(summed[:, :, used - 1], 0)

    return (
        layer_out,
        grad_input,
        grad_gain,
        grad_query,
        grad_key,
        grad_value,
        grad_output,
        grad_value_router,
        grad_output_router,
        grad_route_expert,
        grad_up,
        grad_down,
    )


def solution(mesh):
    both = P(("blk", "head"), None)
    columns = P(None, ("blk", "head"))
    vector = P(("blk", "head"))
    triple = P(("blk", "head"), None, None)
    return jax.shard_map(
        on_device,
        mesh=mesh,
        in_specs=(
            both, both, vector, both, both, both, both, both, both, columns, columns, both,
            triple, triple, both,
        ),
        out_specs=(
            both, both, vector, both, both, both, both, both, both, columns, columns, both,
        ),
        check_vma=False,
    )
```

```python
import functools

import jax
import jax.numpy as jnp
from jax import lax
from jax.experimental import pallas as pl
from jax.experimental.pallas import tpu as pltpu
from jax.sharding import PartitionSpec as P

ATT_BLOCK = 256
ln_eps = 1e-05
rope_base = 10000.0
MIB = 1 << 20
LANES = 128
TILE = 256
BF = jnp.bfloat16
F32 = jnp.float32
VMEM = pl.BlockSpec(memory_space=pltpu.VMEM)
SMEM = pl.BlockSpec(memory_space=pltpu.SMEM)
ANY = pl.BlockSpec(memory_space=pl.ANY)
CHEAP = pl.CostEstimate(flops=0, bytes_accessed=0, transcendentals=0)
PARAMS = pltpu.CompilerParams(vmem_limit_bytes=56 * MIB)


def swap(value, axis, mask):
    size = lax.axis_size(axis)
    return lax.ppermute(value, axis, [(i, i ^ mask) for i in range(size)])


def gather_blk(value):
    far = [value] + [swap(value, "blk", m) for m in range(2, lax.axis_size("blk"), 2)]
    pieces = []
    for mine in far:
        pieces += [mine, swap(mine, "blk", 1)]
    return pieces


def gather_head(value):
    return [value] + [swap(value, "head", m) for m in range(1, lax.axis_size("head"))]


def hold_kernel(*refs):
    del refs


def hold(value, *tokens):
    return pl.pallas_call(
        hold_kernel,
        out_shape=jax.ShapeDtypeStruct(value.shape, value.dtype),
        in_specs=[ANY] * (1 + len(tokens)),
        out_specs=ANY,
        input_output_aliases={0: 0},
        cost_estimate=CHEAP,
        name="hold",
    )(value, *tokens)


def add_low(left, right):
    return (left.astype(F32) + right.astype(F32)).astype(BF)


def shape(dims, dtype):
    return jax.ShapeDtypeStruct(dims, dtype)


def nt(left, right):
    return lax.dot_general(left, right, (((1,), (1,)), ((), ())), preferred_element_type=F32)


def tn(left, right):
    return lax.dot_general(left, right, (((0,), (0,)), ((), ())), preferred_element_type=F32)


def nn(left, right):
    return jnp.dot(left, right, preferred_element_type=F32)


def turn(values, cosine, sine):
    return values * cosine + pltpu.roll(values, values.shape[-1] // 2, 1) * sine


def block_of(place, blk, head, tok_rows, span):
    return (blk * span + (head ^ (place // tok_rows)) * tok_rows + place % tok_rows) // ATT_BLOCK


def own_allowed(blk, head, tok_rows, span):
    keys = lax.broadcasted_iota(jnp.int32, (span, span), 0)
    queries = lax.broadcasted_iota(jnp.int32, (span, span), 1)
    return block_of(keys, blk, head, tok_rows, span) <= block_of(
        queries, blk, head, tok_rows, span
    )


def norm_of(values):
    centre = jnp.mean(values, -1, keepdims=True)
    shifted = values - centre
    inv_std = lax.rsqrt(jnp.mean(shifted * shifted, -1, keepdims=True) + ln_eps)
    return shifted * inv_std, inv_std


def high_low(values):
    high = values.astype(BF)
    return high, (values - high.astype(F32)).astype(BF)


def gain_row(weights_ref, lane, first):
    rows = weights_ref.shape[0]
    parts = []
    for at in range(0, rows, LANES):
        block = weights_ref[at : at + LANES, first : first + LANES].astype(F32)
        parts.append(block.T[lane : lane + 1])
    return jnp.concatenate(parts, axis=1)


def select(rows_of_lane, valid, from_row):
    return (valid & (from_row == rows_of_lane)).astype(BF)


def pack_kernel(layout, q_ref, k_ref, v_ref, rv_ref, ro_ref, gain_ref, ids_ref, tok_ref, out_ref, *copies):
    size, mixed, att, head_count, gain_lane = layout
    row = lax.broadcasted_iota(jnp.int32, (LANES, LANES), 0)
    lane = lax.broadcasted_iota(jnp.int32, (LANES, LANES), 1)
    rows = q_ref.shape[0]
    few = att * head_count
    for copy in copies:
        copy[...] = tok_ref[...]
    small = jnp.concatenate(
        [
            rv_ref[...].astype(F32),
            ro_ref[...].astype(F32),
            gain_ref[...].astype(F32),
            jnp.zeros((LANES - 2 * few - 1, rows), F32),
        ]
    ).astype(BF)
    packed = 2 * size + mixed + LANES
    for h in range(head_count):
        out_ref[h, :rows, :size] = q_ref[:, h * size : (h + 1) * size]
        out_ref[h, :rows, size : 2 * size] = k_ref[:, h * size : (h + 1) * size]
        out_ref[h, :rows, 2 * size : 2 * size + mixed] = v_ref[:, h * mixed : (h + 1) * mixed]
        out_ref[h, : ids_ref.shape[0], packed:] = ids_ref[...].astype(BF)
        part = lane // att - 1
        source = att * head_count + att * (h ^ part) + lane % att
        source = jnp.where(lane < att, att * h + lane, source)
        source = jnp.where(lane == gain_lane, 2 * att * head_count, source)
        tail = tn(small, select(source, lane <= gain_lane, row))
        out_ref[h, :rows, 2 * size + mixed : packed] = tail.astype(BF)


def project_kernel(layout, heads, groups, named, at_ref, cos_ref, sin_ref, ids_ref, *refs):
    tok_refs, w_refs = refs[:heads], refs[heads : heads + groups]
    qkv_ref, values_ref, gate_ref, weight_ref, all_ref, normed_ref = refs[heads + groups :]
    size, mixed, att, head_count, gain_lane = layout
    blk, head = at_ref[0], at_ref[1]
    rows = w_refs[0].shape[0]
    tok_rows = tok_refs[0].shape[0]
    width = normed_ref.shape[1]
    span = normed_ref.shape[0]
    for mask in range(groups):
        start = pl.multiple_of((blk ^ mask) * rows, rows)
        all_ref[pl.ds(start, rows), :] = w_refs[mask][...]
    gain = gain_row(all_ref, gain_lane, 2 * size + mixed)
    for s in range(heads):
        normal, _ = norm_of(tok_refs[s][...].astype(F32))
        normed_ref[s * tok_rows : (s + 1) * tok_rows, :] = (normal * gain).astype(BF)
    pre = nn(normed_ref[...], all_ref[:, : 2 * size])
    cosine, sine = cos_ref[...], sin_ref[...]
    qkv_ref[:span, :size] = turn(pre[:, :size], cosine, sine).astype(BF)
    qkv_ref[:span, size : 2 * size] = turn(pre[:, size:], cosine, sine).astype(BF)
    extra = (qkv_ref.shape[0] - span) // (-(-heads // 3))
    for s in range(heads):
        rows = slice(span + s // 3 * extra, span + (s // 3 + 1) * extra)
        ids = ids_ref[head ^ s, ids_ref.shape[1] - extra :, :]
        qkv_ref[rows, s % 3 * LANES : (s % 3 + 1) * LANES] = ids
    for s in range(heads, -(-heads // 3) * 3):
        rows = slice(span + s // 3 * extra, span + (s // 3 + 1) * extra)
        qkv_ref[rows, s % 3 * LANES : (s % 3 + 1) * LANES] = jnp.zeros((extra, LANES), BF)
    wide = jnp.concatenate([ref[...] for ref in tok_refs])
    marks = []
    for s in range(heads):
        ids = ids_ref[head ^ s].astype(F32)
        ids = jnp.concatenate([ids, jnp.zeros((LANES - ids.shape[0], tok_rows), F32)])
        marks.append(ids.T.astype(BF))
    marks = jnp.concatenate(marks)
    row = lax.broadcasted_iota(jnp.int32, (LANES, LANES), 0)
    lane = lax.broadcasted_iota(jnp.int32, (LANES, LANES), 1)
    column = named * head_count + named * (head ^ (lane // att - 1))
    column = jnp.where(lane < att, named * head, column)
    valid = lane < att * (head_count + 1)
    expert = lax.broadcasted_iota(jnp.int32, (span, LANES), 1)
    inside = expert < att * (head_count + 1)
    expert = (expert % att).astype(F32)
    hot = jnp.zeros((span, LANES), F32)
    for k in range(named):
        ids = nn(marks, select(column + k, valid, row))
        hot = jnp.where(inside & (ids == expert), 1.0, hot)
    gates = jax.nn.sigmoid(nn(wide, all_ref[:, 2 * size + mixed :]))
    weight = hot * gates
    gate_ref[...] = gates
    weight_ref[...] = weight
    value = jnp.zeros((span, size), F32)
    first = 2 * size
    expert_values = nn(wide, all_ref[:, first : first + mixed])
    values_ref[...] = expert_values
    for e in range(att):
        value += weight[:, e : e + 1] * expert_values[:, e * size : (e + 1) * size]
    qkv_ref[:span, 2 * size :] = value.astype(BF)


def attend_kernel(groups, tok_rows, span, scale, at_ref, *refs):
    refs, (o_ref, lse_ref, top_ref, total_ref, acc_ref) = refs[:groups], refs[-5:]
    size = refs[0].shape[1] // 3
    blk, head = at_ref[0], at_ref[1]
    queries = refs[0][:span, :size]

    def advance(ref, first):
        scores = nt(ref[:span, size : 2 * size], queries) * scale
        if first:
            scores = jnp.where(own_allowed(blk, head, tok_rows, span), scores, -jnp.inf)
            top = jnp.max(scores, 0, keepdims=True)
        else:
            top = jnp.maximum(top_ref[...], jnp.max(scores, 0, keepdims=True))
        weights = jnp.exp(scores - top)
        mass = jnp.sum(weights, 0, keepdims=True)
        term = tn(ref[:span, 2 * size :], weights.astype(BF))
        if first:
            total_ref[...] = mass
            acc_ref[...] = term
        else:
            fade = jnp.exp(top_ref[...] - top)
            total_ref[...] = total_ref[...] * fade + mass
            acc_ref[...] = acc_ref[...] * fade + term
        top_ref[...] = top

    advance(refs[0], True)
    for mask in range(1, groups):
        pl.when((blk ^ mask) < blk)(functools.partial(advance, refs[mask], False))
    lse_ref[...] = top_ref[...] + jnp.log(total_ref[...])
    o_ref[...] = (acc_ref[...] / total_ref[...]).T.astype(BF)


def attend(at, qkv, tok_rows, span, scale, tokens):
    size = qkv[0].shape[1] // 3
    groups = len(qkv)
    return pl.pallas_call(
        functools.partial(attend_kernel, groups, tok_rows, span, scale),
        out_shape=(shape((span, size), BF), shape((1, span), F32)),
        in_specs=[SMEM] + [VMEM] * groups + [ANY] * len(tokens),
        out_specs=(VMEM, VMEM),
        scratch_shapes=[
            pltpu.VMEM((1, span), F32),
            pltpu.VMEM((1, span), F32),
            pltpu.VMEM((size, span), F32),
        ],
        compiler_params=PARAMS,
        cost_estimate=CHEAP,
        name="attend",
    )(at, *qkv, *tokens)


def attend_back_kernel(groups, tok_rows, span, scale, at_ref, *refs):
    own_refs, dout_refs = refs[:groups], refs[groups : 2 * groups]
    dq_ref, dk_ref, dv_ref, dq_acc = refs[-4:]
    size = own_refs[0].shape[1] // 3
    blk, head = at_ref[0], at_ref[1]
    parts = span // LANES

    def stat(ref, which):
        first = span + 2 * parts * which
        high = ref[first : first + parts, :].astype(F32)
        low = ref[first + parts : first + 2 * parts, :].astype(F32)
        both = high + low
        return jnp.concatenate([both[i : i + 1] for i in range(parts)], axis=1)

    def terms(key_ref, query_ref, dout_ref, own):
        scores = nt(key_ref[:span, size : 2 * size], query_ref[:span, :size]) * scale
        if own:
            scores = jnp.where(own_allowed(blk, head, tok_rows, span), scores, -jnp.inf)
        prob = jnp.exp(scores - stat(dout_ref, 0))
        prob_grad = nt(key_ref[:span, 2 * size :], dout_ref[:span, :])
        score_grad = prob * (prob_grad - stat(dout_ref, 1)) * scale
        return prob.astype(BF), score_grad.astype(BF)

    prob, grad = terms(own_refs[0], own_refs[0], dout_refs[0], True)
    dq_acc[...] = tn(own_refs[0][:span, size : 2 * size], grad)
    dk_ref[...] = nn(grad, own_refs[0][:span, :size])
    dv_ref[...] = nn(prob, dout_refs[0][:span, :])

    def earlier(mask):
        prob, grad = terms(own_refs[mask], own_refs[0], dout_refs[0], False)
        dq_acc[...] += tn(own_refs[mask][:span, size : 2 * size], grad)

    def later(mask):
        prob, grad = terms(own_refs[0], own_refs[mask], dout_refs[mask], False)
        dk_ref[...] += nn(grad, own_refs[mask][:span, :size])
        dv_ref[...] += nn(prob, dout_refs[mask][:span, :])

    for mask in range(1, groups):
        pl.when((blk ^ mask) < blk)(functools.partial(earlier, mask))
        pl.when((blk ^ mask) > blk)(functools.partial(later, mask))
    dq_ref[...] = dq_acc[...].T


def attend_back(at, qkv, douts, tok_rows, span, scale, tokens):
    size = qkv[0].shape[1] // 3
    groups = len(qkv)
    return pl.pallas_call(
        functools.partial(attend_back_kernel, groups, tok_rows, span, scale),
        out_shape=(shape((span, size), F32),) * 3,
        in_specs=[SMEM] + [VMEM] * (2 * groups) + [ANY] * len(tokens),
        out_specs=(VMEM,) * 3,
        scratch_shapes=[pltpu.VMEM((size, span), F32)],
        compiler_params=PARAMS,
        cost_estimate=CHEAP,
        name="attend_back",
    )(at, *qkv, *douts, *tokens)


def mix_kernel(layout, heads, at_ref, *refs):
    o_refs, tok_refs = refs[:heads], refs[heads : 2 * heads]
    weight_ref, wo_ref = refs[2 * heads : 2 * heads + 2]
    x1_ref, low_ref, u_ref = refs[-3:]
    size, mixed, att, _, _ = layout
    head = at_ref[1]
    span = weight_ref.shape[0]
    tok_rows = span // heads

    @pl.when(pl.program_id(0) == 0)
    def _():
        for s in range(heads):
            start = (head ^ s) * mixed
            for r in range(heads):
                rows = slice(r * tok_rows, (r + 1) * tok_rows)
                there = slice((r ^ s) * tok_rows, ((r ^ s) + 1) * tok_rows)
                out = o_refs[s][there, :].astype(F32)
                for e in range(att):
                    lane = att + att * s + e
                    u_ref[rows, pl.ds(pl.multiple_of(start + e * size, size), size)] = (
                        weight_ref[rows, lane : lane + 1] * out
                    ).astype(BF)

    own = jnp.concatenate([ref[...] for ref in tok_refs]).astype(F32)
    x1 = own + nn(u_ref[...], wo_ref[...])
    x1_ref[...] = x1[:tok_rows]
    low_ref[...] = x1.astype(BF)


def mix(layout, at, outs, tok_pieces, weight, w_output, tokens):
    heads = len(outs)
    span = weight.shape[0]
    depth, width = w_output.shape
    step = min(width, 256)

    def whole(array):
        return pl.BlockSpec(array.shape, lambda i: (0, 0))

    def columns(rows):
        return pl.BlockSpec((rows, step), lambda i: (0, i))

    return pl.pallas_call(
        functools.partial(mix_kernel, layout, heads),
        grid=(width // step,),
        out_shape=(
            shape((span // heads, width), F32),
            shape((span, width), BF),
            shape((span, depth), BF),
        ),
        in_specs=[SMEM]
        + [whole(o) for o in outs]
        + [columns(span // heads)] * heads
        + [whole(weight), columns(depth)]
        + [ANY] * len(tokens),
        out_specs=(
            columns(span // heads),
            columns(span),
            pl.BlockSpec((span, depth), lambda i: (0, 0)),
        ),
        compiler_params=PARAMS,
        cost_estimate=CHEAP,
        name="mix",
    )(at, *outs, *tok_pieces, weight, w_output, *tokens)


SLOTS = 16


def sub_blocks(groups, heads, tok_rows):
    for p in range(groups):
        for s in range(heads):
            sub = p * heads + s
            rows = slice(s * tok_rows, (s + 1) * tok_rows)
            yield p, s, sub, rows, slice(sub * SLOTS, (sub + 1) * SLOTS)


def send_back(groups, heads, tok_rows, experts, slots, back, buf, targets, sems):
    sends = []
    width = buf.shape[2]
    for p, s, sub, rows, at in sub_blocks(groups, heads, tok_rows):
        values = slots[:experts, at, :].reshape(experts * SLOTS, width)
        buf[p, rows, :] = nn(back[sub], values).astype(BF)
        if s == heads - 1:
            move = pltpu.make_async_copy(buf.at[p], targets[p], sems.at[p])
            move.start()
            sends.append(move)
    return sends


def forward_kernel(plan, heads, experts, top, at_ref, *refs):
    chosen, count = plan
    groups = len(chosen)
    x_refs, id_refs = refs[:count], refs[count : count + groups]
    up_hbm, down_hbm, route_ref = refs[count + groups : count + groups + 3]
    outs = refs[count + groups + 3 :]
    out_refs = outs[:groups]
    xs_hbm, hidden_hbm, act_hbm, slope_hbm, here_hbm, back_hbm, gate_ref = outs[groups : groups + 7]
    xbuf, idbuf, xslot, hidden_ref, act_ref, slope_ref, up_ref, down_ref, here_ref, back = outs[
        groups + 7 : groups + 17
    ]
    in_sem, out_sem = outs[groups + 17 :]
    oslot = xbuf
    width = xbuf.shape[2]
    span = sum(x_refs[i].shape[0] for i in chosen[0])
    tok_rows = span // heads
    unit = up_ref.shape[1] // experts
    extra = idbuf.shape[1]
    arrivals = []
    sem = 0
    for p in range(groups):
        moves = []
        row = 0
        for index in chosen[p]:
            size = x_refs[index].shape[0]
            place = xbuf.at[p, pl.ds(row, size)]
            moves.append(pltpu.make_async_copy(x_refs[index], place, in_sem.at[sem]))
            row += size
            sem += 1
        source = id_refs[p].at[pl.ds(span, extra)]
        moves.append(pltpu.make_async_copy(source, idbuf.at[p], in_sem.at[sem]))
        sem += 1
        arrivals.append(moves)
    weights = [
        pltpu.make_async_copy(up_hbm, up_ref, in_sem.at[sem]),
        pltpu.make_async_copy(down_hbm, down_ref, in_sem.at[sem + 1]),
    ]
    for moves in [*arrivals, weights]:
        for move in moves:
            move.start()

    earlier = lax.broadcasted_iota(jnp.int32, (tok_rows, tok_rows), 0)
    later = lax.broadcasted_iota(jnp.int32, (tok_rows, tok_rows), 1)
    before = (earlier < later).astype(BF)
    place = lax.broadcasted_iota(jnp.int32, (experts, SLOTS, tok_rows), 1).astype(F32)
    for p, s, sub, rows, at in sub_blocks(groups, heads, tok_rows):
        if s == 0:
            for move in arrivals[p]:
                move.wait()
        ids = idbuf[p, s // 3 * top : (s // 3 + 1) * top, s % 3 * LANES : (s % 3 + 1) * LANES]
        ids = ids.astype(F32)
        hots = []
        for e in range(experts):
            met = ids == (at_ref[2] + e).astype(F32)
            hots.append(jnp.max(met.astype(F32), 0, keepdims=True))
        hot = jnp.concatenate(hots)
        rank = nn(hot.astype(BF), before)
        rank = jnp.where(hot > 0.0, rank, -1.0)
        here = (rank[:, None, :] == place).astype(F32).reshape(experts * SLOTS, tok_rows)
        back[sub] = here.T.astype(BF)
        here = here.astype(BF)
        here_ref[sub] = here
        moved = nn(here, xbuf[p, rows, :]).astype(BF)
        xslot[:experts, at, :] = moved.reshape(experts, SLOTS, width)
    saves = [
        pltpu.make_async_copy(source, target, out_sem.at[groups + i])
        for i, (source, target) in enumerate(
            (
                (xslot.at[pl.ds(0, experts)], xs_hbm),
                (here_ref, here_hbm),
                (back, back_hbm),
                (hidden_ref, hidden_hbm),
                (act_ref, act_hbm),
                (slope_ref, slope_hbm),
            )
        )
    ]
    for move in saves[:3]:
        move.start()
    for move in weights:
        move.wait()

    route = route_ref[...]
    held = xslot.shape[1]
    lane = lax.broadcasted_iota(jnp.int32, (held, LANES), 1)
    gate_slopes = jnp.zeros((held, LANES), F32)
    for e in range(experts):
        cols = slice(e * unit, (e + 1) * unit)
        both = jnp.concatenate([up_ref[:, cols], route], axis=1)
        pre_all = nn(xslot[e], both)
        pre, gate = pre_all[:, :unit], jax.nn.sigmoid(pre_all[:, unit + e : unit + e + 1])
        sig = jax.nn.sigmoid(pre)
        act = pre * sig
        hidden = (act * gate).astype(BF)
        hidden_ref[e] = hidden
        act_ref[e] = act
        slope_ref[e] = gate * (sig + act * (1.0 - sig))
        gate_slopes = jnp.where(lane == e, gate * (1.0 - gate), gate_slopes)
        oslot[e] = nn(hidden, down_ref[cols, :]).astype(BF)
    gate_ref[...] = gate_slopes
    for move in saves[3:]:
        move.start()
    saves[0].wait()
    sends = send_back(
        groups, heads, tok_rows, experts, oslot, back, xslot, out_refs, out_sem
    )
    for move in [*saves[1:], *sends]:
        move.wait()


def back_kernel(far, groups, heads, experts, at_ref, *refs):
    g_hbm, up_hbm, down_hbm, act_hbm, slope_hbm, here_hbm, back_hbm = refs[:7]
    route_ref, gate_ref = refs[7:9]
    dx_refs, (gs_hbm, da_ref) = refs[9 : 9 + groups], refs[9 + groups : 11 + groups]
    gbuf, gslot, dslot, act_ref, slope_ref, up_ref, down_ref, here_ref, back = refs[
        11 + groups : 20 + groups
    ]
    in_sem, out_sem = refs[20 + groups :]
    tok_rows, width = gbuf.shape[2:]
    unit = up_ref.shape[1] // experts
    arrivals = [
        [
            pltpu.make_async_copy(source, target, in_sem.at[i])
            for i, (source, target) in enumerate(
                (
                    (here_hbm, here_ref),
                    (down_hbm, down_ref),
                    (act_hbm, act_ref),
                    (slope_hbm, slope_ref),
                    (up_hbm, up_ref),
                    (back_hbm, back),
                )
            )
        ]
    ]
    sem = len(arrivals[0])
    for p in range(groups):
        moves = []
        for s in range(heads):
            device = (at_ref[0] ^ (far + p)) * heads + (at_ref[1] ^ s)
            source = g_hbm.at[pl.ds(pl.multiple_of(device * tok_rows, tok_rows), tok_rows)]
            moves.append(pltpu.make_async_copy(source, gbuf.at[p, s], in_sem.at[sem]))
            sem += 1
        arrivals.append(moves)
    arrivals[0][0].start()
    for moves in arrivals[1:]:
        for move in moves:
            move.start()
    for move in arrivals[0][1:]:
        move.start()
    arrivals[0][0].wait()
    for p, s, sub, rows, at in sub_blocks(groups, heads, tok_rows):
        if s == 0:
            for move in arrivals[1 + p]:
                move.wait()
        moved = nn(here_ref[sub], gbuf[p, s]).astype(BF)
        gslot[:experts, at, :] = moved.reshape(experts, SLOTS, width)
    save = pltpu.make_async_copy(gslot.at[pl.ds(0, experts)], gs_hbm, out_sem.at[groups])
    save.start()
    for move in arrivals[0][1:]:
        move.wait()
    route = route_ref[...]
    held = gslot.shape[1]
    lane = lax.broadcasted_iota(jnp.int32, (held, LANES), 1)
    for e in range(experts):
        cols = slice(e * unit, (e + 1) * unit)
        both = jnp.concatenate([up_ref[:, cols], route], axis=1)
        dh = nt(gslot[e], down_ref[cols, :])
        da = (dh * slope_ref[e]).astype(BF)
        dsm = jnp.sum(dh * act_ref[e], -1, keepdims=True) * gate_ref[...]
        dsm = jnp.where(lane == e, dsm, 0.0).astype(BF)
        da = jnp.concatenate([da, dsm], axis=1)
        da_ref[e] = da
        dslot[e] = nt(da, both).astype(BF)
    save.wait()
    sends = send_back(groups, heads, tok_rows, experts, dslot, back, gslot, dx_refs, out_sem)
    for move in sends:
        move.wait()


def run_experts(at, far, xs, ids, g_all, up, down, route, experts, top, heads):
    groups = len(xs)
    width, units = up.shape
    unit = units // experts
    span = sum(x.shape[0] for x in xs[0])
    tok_rows = span // heads
    held = groups * heads * SLOTS
    chosen, flat = [], []
    for arrays in xs:
        chosen.append(tuple(range(len(flat), len(flat) + len(arrays))))
        flat += arrays
    subs = groups * heads
    slots = pltpu.VMEM((max(experts, groups), max(held, span), width), BF)
    dims = {
        "rows": ((experts, held, width), BF),
        "hidden": ((experts, held, unit), BF),
        "wide": ((experts, held, unit), F32),
        "here": ((subs, experts * SLOTS, tok_rows), BF),
        "back": ((subs, tok_rows, experts * SLOTS), BF),
    }
    vm = {name: pltpu.VMEM(*dim) for name, dim in dims.items()}
    hbm = {name: shape(*dim) for name, dim in dims.items()}
    both = [pltpu.VMEM((width, units), BF), pltpu.VMEM((units, width), BF)]
    params = pltpu.CompilerParams(vmem_limit_bytes=58 * MIB)
    done = pl.pallas_call(
        functools.partial(forward_kernel, (chosen, len(flat)), heads, experts, top),
        out_shape=(shape((span, width), BF),) * groups
        + (hbm["rows"], hbm["hidden"], hbm["wide"], hbm["wide"], hbm["here"], hbm["back"])
        + (shape((held, LANES), F32),),
        in_specs=[SMEM] + [ANY] * (len(flat) + groups + 2) + [VMEM],
        out_specs=(ANY,) * (groups + 6) + (VMEM,),
        scratch_shapes=[
            slots,
            pltpu.VMEM((groups, ids[0].shape[0] - span, ids[0].shape[1]), BF),
            slots,
            vm["hidden"],
            vm["wide"],
            vm["wide"],
            *both,
            vm["here"],
            vm["back"],
            pltpu.SemaphoreType.DMA((len(flat) + groups + 2,)),
            pltpu.SemaphoreType.DMA((groups + 6,)),
        ],
        compiler_params=params,
        cost_estimate=CHEAP,
        name="experts_forward",
    )(at, *flat, *ids, up, down, route)
    outs, (rows, hidden, act, slope, here, back, gates) = done[:groups], done[groups:]
    done = pl.pallas_call(
        functools.partial(back_kernel, far, groups, heads, experts),
        out_shape=(shape((span, width), BF),) * groups
        + (hbm["rows"], shape((experts, held, unit + LANES), BF)),
        in_specs=[SMEM] + [ANY] * 7 + [VMEM, VMEM],
        out_specs=(ANY,) * (groups + 1) + (VMEM,),
        scratch_shapes=[
            pltpu.VMEM((groups, heads, tok_rows, width), BF),
            slots,
            vm["rows"],
            vm["wide"],
            vm["wide"],
            *both,
            vm["here"],
            vm["back"],
            pltpu.SemaphoreType.DMA((6 + subs,)),
            pltpu.SemaphoreType.DMA((groups + 1,)),
        ],
        compiler_params=params,
        cost_estimate=CHEAP,
        name="experts_back",
    )(at, g_all, up, down, act, slope, here, back, route, gates)
    return outs, done[:groups], (rows, done[groups], hidden, done[groups + 1])


def expert_grads_kernel(halves, *refs):
    x_refs, g_refs, hidden_refs, da_refs = (
        refs[i * halves : (i + 1) * halves] for i in range(4)
    )
    up_ref, down_ref, route_ref = refs[-3:]
    unit = up_ref.shape[1]
    up = down = None
    for x_ref, g_ref, hidden_ref, da_ref in zip(x_refs, g_refs, hidden_refs, da_refs):
        term = tn(x_ref[0], da_ref[0])
        up = term if up is None else up + term
        term = tn(hidden_ref[0], g_ref[0])
        down = term if down is None else down + term
    up_ref[...] = up[:, :unit]
    down_ref[...] = down

    @pl.when(pl.program_id(0) == 0)
    def _():
        route_ref[...] = up[:, unit:]

    @pl.when(pl.program_id(0) > 0)
    def _():
        route_ref[...] += up[:, unit:]


def expert_grads(results, tokens):
    halves = len(results)
    experts, held, width = results[0][0].shape
    unit = results[0][2].shape[2]

    def block(array):
        return pl.BlockSpec((1,) + array.shape[1:], lambda e: (e, 0, 0))

    flat = [result[i] for i in range(4) for result in results]
    return pl.pallas_call(
        functools.partial(expert_grads_kernel, halves),
        grid=(experts,),
        out_shape=(
            shape((width, experts * unit), F32),
            shape((experts * unit, width), F32),
            shape((width, LANES), F32),
        ),
        in_specs=[block(array) for array in flat] + [ANY] * len(tokens),
        out_specs=(
            pl.BlockSpec((width, unit), lambda e: (0, e)),
            pl.BlockSpec((unit, width), lambda e: (e, 0)),
            pl.BlockSpec((width, LANES), lambda e: (0, 0)),
        ),
        compiler_params=PARAMS,
        cost_estimate=CHEAP,
        name="expert_grads",
    )(*flat, *tokens)


def spread_kernel(layout, heads, terms, at_ref, *refs):
    term_refs = refs[:terms]
    grad_ref, wo_ref, weight_ref = refs[terms : terms + 3]
    o_refs = refs[terms + 3 : terms + 3 + heads]
    g1_ref, low_ref = refs[-2 - heads : -heads]
    send_refs = refs[-heads:]
    size, mixed, att, _, _ = layout
    head = at_ref[1]
    span = g1_ref.shape[0]
    tok_rows = span // heads
    total = term_refs[0][...].astype(F32)
    for ref in term_refs[1:]:
        total += ref[...].astype(F32)
    g1_ref[...] = total
    g1_ref[:tok_rows, :] += grad_ref[...].astype(F32)
    low_ref[...] = g1_ref[...].astype(BF)
    lane = lax.broadcasted_iota(jnp.int32, (tok_rows, LANES), 1)
    for s in range(heads):
        start = pl.multiple_of((head ^ s) * mixed, LANES)
        du = nt(low_ref[...], wo_ref[pl.ds(start, mixed), :])
        for r in range(heads):
            rows = slice(r * tok_rows, (r + 1) * tok_rows)
            there = slice((r ^ s) * tok_rows, ((r ^ s) + 1) * tok_rows)
            out = o_refs[s][there, :].astype(F32)
            dout = jnp.zeros((tok_rows, size), F32)
            dots = jnp.zeros((tok_rows, LANES), F32)
            for e in range(att):
                at = att + att * s + e
                term = du[rows, e * size : (e + 1) * size]
                dout += weight_ref[rows, at : at + 1] * term
                dots = jnp.where(lane == e, jnp.sum(term * out, -1, keepdims=True), dots)
            send_refs[s][there, :] = dout.astype(BF)
            high, low = high_low(dots.T[:8, :])
            first = span + 16 * (r ^ s)
            send_refs[s][first : first + 16, :] = jnp.concatenate([high, low])


def spread(layout, at, terms, out_grad, w_output, weight, outs, tokens):
    heads = len(outs)
    span, width = terms[0].shape
    tok_rows = span // heads
    size = outs[0].shape[1]
    return pl.pallas_call(
        functools.partial(spread_kernel, layout, heads, len(terms)),
        out_shape=(shape((span, width), F32), shape((span, width), BF))
        + (shape((span + 16 * heads, size), BF),) * heads,
        in_specs=[SMEM] + [VMEM] * (len(terms) + 3 + heads) + [ANY] * len(tokens),
        out_specs=(VMEM,) * (2 + heads),
        compiler_params=PARAMS,
        cost_estimate=CHEAP,
        name="spread",
    )(at, *terms, out_grad, w_output, weight, *outs, *tokens)


def join_kernel(heads, att, *refs):
    got_refs, (o_ref, lse_ref, gate_ref, weight_ref) = refs[:heads], refs[heads : heads + 4]
    dout_ref, dso_ref = refs[-2:]
    span, size = o_ref.shape
    tok_rows = span // heads
    parts = span // LANES
    total = got_refs[0][...].astype(F32)
    for ref in got_refs[1:]:
        total += ref[...].astype(F32)
    low = total[:span].astype(BF)
    dout_ref[:span, :] = low
    product = low.astype(F32) * o_ref[...].astype(F32)
    stats = []
    lse = lse_ref[...]
    rows = [lse[:, i * LANES : (i + 1) * LANES] for i in range(parts)]
    stats += high_low(jnp.concatenate(rows))
    rows = [
        jnp.sum(product[i * LANES : (i + 1) * LANES].T, 0, keepdims=True) for i in range(parts)
    ]
    stats += high_low(jnp.concatenate(rows))
    dout_ref[span:, :] = jnp.concatenate(stats)
    for r in range(heads):
        first = span + 16 * r
        sums = total[first : first + 8] + total[first + 8 : first + 16]
        sums = jnp.concatenate([sums, jnp.zeros((LANES - 8, LANES), F32)]).T
        rows = slice(r * tok_rows, (r + 1) * tok_rows)
        moved = pltpu.roll(sums, att, 1)
        dso_ref[rows, :] = (moved * weight_ref[rows, :] * (1.0 - gate_ref[rows, :])).astype(BF)


def join(got, mine, log_total, gate, weight, att, tokens):
    heads = len(got)
    span, size = mine.shape
    parts = span // LANES
    return pl.pallas_call(
        functools.partial(join_kernel, heads, att),
        out_shape=(shape((span + 4 * parts, size), BF), shape((span, LANES), BF)),
        in_specs=[VMEM] * (heads + 4) + [ANY] * len(tokens),
        out_specs=(VMEM, VMEM),
        compiler_params=PARAMS,
        cost_estimate=CHEAP,
        name="join",
    )(*got, mine, log_total, gate, weight, *tokens)


def output_grad_kernel(rows, groups, at_ref, u_ref, g_ref, even_ref, odd_ref, all_ref):
    all_ref[...] = tn(u_ref[...], g_ref[...]).astype(BF)
    for mask in range(groups):
        place = pl.ds(pl.multiple_of((at_ref[0] ^ mask) * rows, rows), rows)
        ref = odd_ref if mask % 2 else even_ref
        ref[mask // 2 * rows : (mask // 2 + 1) * rows, :] = all_ref[place, :]


def output_grad(at, u, g, groups):
    depth, width = u.shape[1], g.shape[1]
    half = shape((depth // 2, width), BF)
    return pl.pallas_call(
        functools.partial(output_grad_kernel, depth // groups, groups),
        out_shape=(half, half),
        in_specs=[SMEM, VMEM, VMEM],
        out_specs=(VMEM, VMEM),
        scratch_shapes=[pltpu.VMEM((depth, width), BF)],
        compiler_params=PARAMS,
        cost_estimate=CHEAP,
        name="output_grad",
    )(at, u, g)


def branch_kernel(heads, *refs):
    x1_ref, own_ref, send_refs = refs[0], refs[-heads], refs[1 - heads :]
    rows = x1_ref.shape[0]
    for s in range(heads):
        at = slice(s * rows, (s + 1) * rows)
        total = sum(ref[at, :].astype(F32) for ref in refs[1:-heads])
        if s == 0:
            own_ref[...] = x1_ref[...] + total
        else:
            send_refs[s - 1][...] = total.astype(BF)


def branch(x1, terms, heads):
    return pl.pallas_call(
        functools.partial(branch_kernel, heads),
        out_shape=(shape(x1.shape, F32),) + (shape(x1.shape, BF),) * (heads - 1),
        in_specs=[VMEM] * (1 + len(terms)),
        out_specs=(VMEM,) * heads,
        compiler_params=PARAMS,
        cost_estimate=CHEAP,
        name="branch",
    )(x1, *terms)


def finish_kernel(layout, heads, groups, at_ref, *refs):
    (
        dq_ref, dk_ref, dv_ref, cos_ref, sin_ref, values_ref, gate_ref, weight_ref, dso_ref,
        normed_ref, all_ref, g1_ref,
    ) = refs[:12]
    tok_refs = refs[12 : 12 + heads]
    part_refs = refs[-4 - heads : -4]
    even_ref, odd_ref, product_ref, all_grads = refs[-4:]
    size, mixed, att, _, gain_lane = layout
    blk = at_ref[0]
    span, width = normed_ref.shape
    tok_rows = span // heads
    cosine, sine = cos_ref[...], -sin_ref[...]
    query_back = turn(dq_ref[...], cosine, sine).astype(BF)
    key_back = turn(dk_ref[...], cosine, sine).astype(BF)
    qk_back = jnp.concatenate([query_back, key_back], axis=1)
    value_back = dv_ref[...].astype(BF).astype(F32)
    lane = lax.broadcasted_iota(jnp.int32, (span, LANES), 1)
    dots = jnp.zeros((span, LANES), F32)
    columns = []
    for e in range(att):
        columns.append((weight_ref[:, e : e + 1] * value_back).astype(BF))
        dot = jnp.sum(value_back * values_ref[:, e * size : (e + 1) * size], -1, keepdims=True)
        dots = jnp.where(lane == e, dot, dots)
    gates = gate_ref[...]
    tail = (dots * weight_ref[...] * (1.0 - gates)).astype(BF)
    tail = jnp.where(lane < att, tail, jnp.where(lane < 2 * att, dso_ref[...], jnp.zeros_like(tail)))
    v_back = jnp.concatenate(columns + [tail], axis=1)
    gain = gain_row(all_ref, gain_lane, 2 * size + mixed)
    grad_normed = nt(qk_back, all_ref[:, : 2 * size])
    grad_wide = nt(v_back, all_ref[:, 2 * size :])
    for s in range(heads):
        rows = slice(s * tok_rows, (s + 1) * tok_rows)
        normal, inv_std = norm_of(tok_refs[s][...].astype(F32))
        product_ref[rows, :] = (grad_normed[rows] * normal).astype(BF)
        grad_normal = grad_normed[rows] * gain
        part = (
            g1_ref[rows, :]
            + grad_wide[rows]
            + inv_std
            * (
                grad_normal
                - jnp.mean(grad_normal, -1, keepdims=True)
                - normal * jnp.mean(grad_normal * normal, -1, keepdims=True)
            )
        )
        part_refs[s][...] = part if s == 0 else part.astype(BF)
    own = width // groups
    gain_pick = (lane == gain_lane).astype(BF)
    wide = jnp.concatenate([ref[...] for ref in tok_refs])
    all_grads[:, : 2 * size] = tn(normed_ref[...], qk_back).astype(BF)
    from_tokens = tn(wide, v_back)
    all_grads[:, 2 * size : 2 * size + mixed] = from_tokens[:, :mixed].astype(BF)
    all_grads[:, 2 * size + mixed :] = (
        from_tokens[:, mixed:] + tn(product_ref[...], gain_pick)
    ).astype(BF)
    for mask in range(groups):
        place = pl.ds(pl.multiple_of((blk ^ mask) * own, own), own)
        ref = odd_ref if mask % 2 else even_ref
        ref[mask // 2 * own : (mask // 2 + 1) * own, :] = all_grads[place, :]


def finish(layout, heads, groups, at, tokens, *arrays):
    span, width = arrays[9].shape
    packed = arrays[10].shape[1]
    half = (width // 2, packed)
    return pl.pallas_call(
        functools.partial(finish_kernel, layout, heads, groups),
        out_shape=(shape((span // heads, width), F32),)
        + (shape((span // heads, width), BF),) * (heads - 1)
        + (shape(half, BF), shape(half, BF)),
        in_specs=[SMEM] + [VMEM] * len(arrays) + [ANY] * len(tokens),
        out_specs=(VMEM,) * (heads + 2),
        scratch_shapes=[pltpu.VMEM((span, width), BF), pltpu.VMEM((width, packed), BF)],
        compiler_params=PARAMS,
        cost_estimate=CHEAP,
        name="finish",
    )(at, *arrays, *tokens)


def on_device(
    tokens,
    out_grad,
    ln_gain,
    w_query,
    w_key,
    w_value,
    w_output,
    route_value,
    route_output,
    route_expert,
    w_up,
    w_down,
    value_ids,
    output_ids,
    expert_ids,
):
    groups, heads = lax.axis_size("blk"), lax.axis_size("head")
    blk, head = lax.axis_index("blk"), lax.axis_index("head")
    tok_rows, width = tokens.shape
    head_count, named = value_ids.shape[1:]
    att = route_value.shape[1] // head_count
    size = w_query.shape[1] // head_count
    experts = route_expert.shape[1]
    top = expert_ids.shape[1]
    span = tok_rows * heads
    own_rows = w_query.shape[0]
    mixed = att * size
    scale = size ** (-0.5)
    device = blk * heads + head
    at = jnp.stack([blk, head, device * experts]).astype(jnp.int32)
    gain_lane = att + head_count * att
    layout = (size, mixed, att, head_count, gain_lane)
    used = 2 * size + mixed + gain_lane + 1
    packed = 2 * size + mixed + LANES

    ids_rows = 2 * named * head_count + top
    ids = jnp.concatenate(
        [
            value_ids.transpose(1, 2, 0).reshape(-1, tok_rows),
            output_ids.transpose(1, 2, 0).reshape(-1, tok_rows),
            expert_ids.T,
        ]
    )
    by_head, second, third = pl.pallas_call(
        functools.partial(pack_kernel, layout),
        out_shape=(
            shape((head_count, max(own_rows, ids_rows), packed + tok_rows), BF),
            shape(tokens.shape, BF),
            shape(tokens.shape, BF),
        ),
        in_specs=[VMEM] * 8,
        out_specs=(VMEM,) * 3,
        compiler_params=PARAMS,
        name="pack",
    )(w_query, w_key, w_value, route_value.T, route_output.T, ln_gain[None], ids, tokens)
    tok_pieces = [tokens, swap(tokens, "head", 1)]
    by_head = lax.all_to_all(by_head, "head", 0, 0, tiled=True)
    third = hold(third, by_head)
    for mask in range(2, heads):
        tok_pieces.append(swap(second if mask == 2 else third, "head", mask))
    ids_group = by_head[:, :ids_rows, packed:]
    w_pieces = gather_blk(by_head[:, :own_rows, :packed].reshape(heads * own_rows, packed))

    wo_full = lax.all_gather(w_output, ("blk", "head"), axis=0, tiled=True)

    places = jnp.arange(span)
    places = blk * span + (head ^ (places // tok_rows)) * tok_rows + places % tok_rows
    half = size // 2
    frequency = rope_base ** (-jnp.arange(half, dtype=F32) / half)
    angles = places.astype(F32)[:, None] * frequency[None, :]
    cosine, sine = jnp.cos(angles), jnp.sin(angles)
    cosine = jnp.concatenate([cosine, cosine], axis=1)
    sine = jnp.concatenate([-sine, sine], axis=1)

    qkv, expert_values, gate, weight, weights, normed = pl.pallas_call(
        functools.partial(project_kernel, layout, heads, groups, named),
        out_shape=(
            shape((span + -(-heads // 3) * top, 3 * size), BF),
            shape((span, mixed), F32),
            shape((span, LANES), F32),
            shape((span, LANES), F32),
            shape((width, packed), BF),
            shape((span, width), BF),
        ),
        in_specs=[SMEM] + [VMEM] * (3 + heads + groups),
        out_specs=(VMEM,) * 6,
        compiler_params=PARAMS,
        cost_estimate=CHEAP,
        name="project",
    )(at, cosine, sine, ids_group, *tok_pieces, *w_pieces)

    g_all = lax.all_gather(hold(out_grad, qkv), ("blk", "head"), axis=0, tiled=True)

    qkv_pieces = gather_blk(qkv)
    mine, log_total = attend(at, qkv_pieces, tok_rows, span, scale, [])
    outs = gather_head(mine)
    x1, middle, mixed_heads = mix(layout, at, outs, tok_pieces, weight, wo_full, [])

    route = jnp.pad(route_expert, ((0, 0), (0, LANES - experts)))
    near = 8
    branch_terms = grad_terms = weight_grads = None

    def pair_sum(parts, mask):
        return add_low(parts[mask], swap(parts[mask + 1], "blk", 1))

    for far in range(0, groups, near):
        base = middle
        if far:
            base, *old = lax.optimization_barrier(
                (base, branch_terms, grad_terms, *weight_grads)
            )
            branch_terms, grad_terms, *weight_grads = old
            base = swap(base, "blk", far)
        even = {0: [base], 2: [swap(base, "blk", 2)], 4: [swap(base, "blk", 4)]}
        even[6] = [
            swap(even[2][0][: span // 2], "blk", 4),
            swap(even[4][0][span // 2 :], "blk", 2),
        ]
        xs = []
        for mask in range(0, near, 2):
            xs += [even[mask], [swap(x, "blk", 1) for x in even[mask]]]
        outs_all, dxs_all, saved = run_experts(
            at, far, xs, qkv_pieces[far : far + near], g_all, w_up, w_down, route,
            experts, top, heads,
        )
        sums = [pair_sum(dxs_all, m) for m in (2, 4, 6)]
        grad_round = [dxs_all[0], swap(dxs_all[1], "blk", 1)]
        grad_round += [swap(value, "blk", m) for m, value in zip((2, 4, 6), sums)]
        terms = expert_grads([saved], sums)
        out_sums = [hold(pair_sum(outs_all, m), sums[-1]) for m in (2, 4, 6)]
        branch_round = [outs_all[0], swap(outs_all[1], "blk", 1)]
        out_sums = [hold(value, grad_round[-1]) for value in out_sums]
        branch_round += [swap(value, "blk", m) for m, value in zip((2, 4, 6), out_sums)]
        if groups > near:
            def whole(terms):
                return functools.reduce(lambda a, b: a + b, [t.astype(F32) for t in terms])

            out_sum, dx_sum = whole(branch_round), whole(grad_round)
            if far:
                out_sum = branch_terms + swap(out_sum.astype(BF), "blk", far).astype(F32)
                dx_sum = grad_terms + swap(dx_sum.astype(BF), "blk", far).astype(F32)
                weight_grads = [old + new for old, new in zip(weight_grads, terms)]
            else:
                weight_grads = terms
            branch_terms, grad_terms = out_sum, dx_sum
        else:
            branch_terms, grad_terms, weight_grads = branch_round, grad_round, terms
    early = [*out_sums, weight_grads[2]]
    arrived = branch_round[2:]
    if groups > near:
        branch_terms, grad_terms = [branch_terms], [grad_terms]
    grad_up, grad_down, grad_route_expert = weight_grads
    grad_route_expert = grad_route_expert[:, :experts]

    g1, g1_low, *sends = spread(layout, at, grad_terms, out_grad, wo_full, weight, outs, early)
    even, odd = output_grad(at, mixed_heads, g1_low, groups)
    got = [sends[0]] + [swap(sends[m], "head", m) for m in range(1, heads)]
    dout, dso = join(got, mine, log_total, gate, weight, att, [odd])
    dout_pieces = gather_blk(hold(dout, *arrived[:2]))
    layer_out, *outputs = branch(x1, branch_terms, heads)
    pair_sums = add_low(even, swap(hold(odd, *arrived), "blk", 1))
    dq, dk, dv = attend_back(
        at, qkv_pieces, dout_pieces, tok_rows, span, scale, [outputs[0], pair_sums]
    )

    out_rows = w_output.shape[0]
    there = []
    pair_sums = pair_sums.reshape(groups // 2, heads * out_rows, width)
    rows_sum = pair_sums[0].astype(F32)
    for index in range(1, groups // 2):
        got_rows = swap(pair_sums[index], "blk", 2 * index)
        there.append(got_rows)
        rows_sum = rows_sum + got_rows.astype(F32)
    rows_sum = rows_sum.reshape(heads, out_rows, width)
    grad_output = lax.dynamic_index_in_dim(rows_sum, head, 0, keepdims=False)
    for mask in range(1, heads):
        part = lax.dynamic_index_in_dim(rows_sum, head ^ mask, 0, keepdims=False).astype(BF)
        grad_output = grad_output + swap(part, "head", mask).astype(F32)
        got_rows = swap(outputs[mask - 1], "head", mask)
        there.append(got_rows)
        layer_out = layer_out + got_rows.astype(F32)

    grad_input, *parts, even_rows, odd_rows = finish(
        layout, heads, groups, at, there, dq, dk, dv, cosine, sine, expert_values, gate, weight, dso,
        normed, weights, g1, *tok_pieces,
    )
    pairs = add_low(even_rows, swap(odd_rows, "blk", 1))
    own = width // groups
    summed = pairs[:own].astype(F32)
    for index in range(1, groups // 2):
        piece = pairs[index * own : (index + 1) * own]
        summed = summed + swap(piece, "blk", 2 * index).astype(F32)
    for mask in range(1, heads):
        grad_input = grad_input + swap(parts[mask - 1], "head", mask).astype(F32)
    summed = lax.all_to_all(
        summed.astype(BF).reshape(heads, own_rows, packed), "head", 0, 0, tiled=True
    ).astype(F32)

    def columns(first, count):
        return summed[:, :, first : first + count].transpose(1, 0, 2).reshape(own_rows, -1)

    grad_query = columns(0, size)
    grad_key = columns(size, size)
    grad_value = columns(2 * size, mixed)
    grad_value_router = columns(2 * size + mixed, att)
    grad_output_router = columns(2 * size + mixed + att, att)
    grad_gain = jnp.sum(summed[:, :, used - 1], 0)

    return (
        layer_out,
        grad_input,
        grad_gain,
        grad_query,
        grad_key,
        grad_value,
        grad_output,
        grad_value_router,
        grad_output_router,
        grad_route_expert,
        grad_up,
        grad_down,
    )


def solution(mesh):
    both = P(("blk", "head"), None)
    columns = P(None, ("blk", "head"))
    vector = P(("blk", "head"))
    triple = P(("blk", "head"), None, None)
    return jax.shard_map(
        on_device,
        mesh=mesh,
        in_specs=(
            both, both, vector, both, both, both, both, both, both, columns, columns, both,
            triple, triple, both,
        ),
        out_specs=(
            both, both, vector, both, both, both, both, both, both, columns, columns, both,
        ),
        check_vma=False,
    )
```

```python
import functools

import jax
import jax.numpy as jnp
from jax import lax
from jax.experimental import pallas as pl
from jax.experimental.pallas import tpu as pltpu
from jax.sharding import PartitionSpec as P

ATT_BLOCK = 256
ln_eps = 1e-05
rope_base = 10000.0
MIB = 1 << 20
LANES = 128
TILE = 256
BF = jnp.bfloat16
F32 = jnp.float32
VMEM = pl.BlockSpec(memory_space=pltpu.VMEM)
SMEM = pl.BlockSpec(memory_space=pltpu.SMEM)
ANY = pl.BlockSpec(memory_space=pl.ANY)
CHEAP = pl.CostEstimate(flops=0, bytes_accessed=0, transcendentals=0)
PARAMS = pltpu.CompilerParams(vmem_limit_bytes=56 * MIB)


def swap(value, axis, mask):
    size = lax.axis_size(axis)
    return lax.ppermute(value, axis, [(i, i ^ mask) for i in range(size)])


def gather_blk(value):
    far = [value] + [swap(value, "blk", m) for m in range(2, lax.axis_size("blk"), 2)]
    pieces = []
    for mine in far:
        pieces += [mine, swap(mine, "blk", 1)]
    return pieces


def gather_head(value):
    return [value] + [swap(value, "head", m) for m in range(1, lax.axis_size("head"))]


def hold_kernel(*refs):
    del refs


def hold(value, *tokens):
    return pl.pallas_call(
        hold_kernel,
        out_shape=jax.ShapeDtypeStruct(value.shape, value.dtype),
        in_specs=[ANY] * (1 + len(tokens)),
        out_specs=ANY,
        input_output_aliases={0: 0},
        cost_estimate=CHEAP,
        name="hold",
    )(value, *tokens)


def add_low(left, right):
    return (left.astype(F32) + right.astype(F32)).astype(BF)


def shape(dims, dtype):
    return jax.ShapeDtypeStruct(dims, dtype)


def nt(left, right):
    return lax.dot_general(left, right, (((1,), (1,)), ((), ())), preferred_element_type=F32)


def tn(left, right):
    return lax.dot_general(left, right, (((0,), (0,)), ((), ())), preferred_element_type=F32)


def nn(left, right):
    return jnp.dot(left, right, preferred_element_type=F32)


def turn(values, cosine, sine):
    return values * cosine + pltpu.roll(values, values.shape[-1] // 2, 1) * sine


def block_of(place, blk, head, tok_rows, span):
    return (blk * span + (head ^ (place // tok_rows)) * tok_rows + place % tok_rows) // ATT_BLOCK


def own_allowed(blk, head, tok_rows, span):
    keys = lax.broadcasted_iota(jnp.int32, (span, span), 0)
    queries = lax.broadcasted_iota(jnp.int32, (span, span), 1)
    return block_of(keys, blk, head, tok_rows, span) <= block_of(
        queries, blk, head, tok_rows, span
    )


def norm_of(values):
    centre = jnp.mean(values, -1, keepdims=True)
    shifted = values - centre
    inv_std = lax.rsqrt(jnp.mean(shifted * shifted, -1, keepdims=True) + ln_eps)
    return shifted * inv_std, inv_std


def high_low(values):
    high = values.astype(BF)
    return high, (values - high.astype(F32)).astype(BF)


def gain_row(weights_ref, lane, first):
    rows = weights_ref.shape[0]
    parts = []
    for at in range(0, rows, LANES):
        block = weights_ref[at : at + LANES, first : first + LANES].astype(F32)
        parts.append(block.T[lane : lane + 1])
    return jnp.concatenate(parts, axis=1)


def select(rows_of_lane, valid, from_row):
    return (valid & (from_row == rows_of_lane)).astype(BF)


def pack_kernel(layout, q_ref, k_ref, v_ref, rv_ref, ro_ref, gain_ref, ids_ref, tok_ref, out_ref, *copies):
    size, mixed, att, head_count, gain_lane = layout
    row = lax.broadcasted_iota(jnp.int32, (LANES, LANES), 0)
    lane = lax.broadcasted_iota(jnp.int32, (LANES, LANES), 1)
    rows = q_ref.shape[0]
    few = att * head_count
    for copy in copies:
        copy[...] = tok_ref[...]
    small = jnp.concatenate(
        [
            rv_ref[...].astype(F32),
            ro_ref[...].astype(F32),
            gain_ref[...].astype(F32),
            jnp.zeros((LANES - 2 * few - 1, rows), F32),
        ]
    ).astype(BF)
    packed = 2 * size + mixed + LANES
    for h in range(head_count):
        out_ref[h, :rows, :size] = q_ref[:, h * size : (h + 1) * size]
        out_ref[h, :rows, size : 2 * size] = k_ref[:, h * size : (h + 1) * size]
        out_ref[h, :rows, 2 * size : 2 * size + mixed] = v_ref[:, h * mixed : (h + 1) * mixed]
        out_ref[h, : ids_ref.shape[0], packed:] = ids_ref[...].astype(BF)
        part = lane // att - 1
        source = att * head_count + att * (h ^ part) + lane % att
        source = jnp.where(lane < att, att * h + lane, source)
        source = jnp.where(lane == gain_lane, 2 * att * head_count, source)
        tail = tn(small, select(source, lane <= gain_lane, row))
        out_ref[h, :rows, 2 * size + mixed : packed] = tail.astype(BF)


def project_kernel(layout, heads, groups, named, at_ref, cos_ref, sin_ref, ids_ref, *refs):
    tok_refs, w_refs = refs[:heads], refs[heads : heads + groups]
    qkv_ref, values_ref, gate_ref, weight_ref, all_ref, normed_ref = refs[heads + groups :]
    size, mixed, att, head_count, gain_lane = layout
    blk, head = at_ref[0], at_ref[1]
    rows = w_refs[0].shape[0]
    tok_rows = tok_refs[0].shape[0]
    width = normed_ref.shape[1]
    span = normed_ref.shape[0]
    for mask in range(groups):
        start = pl.multiple_of((blk ^ mask) * rows, rows)
        all_ref[pl.ds(start, rows), :] = w_refs[mask][...]
    gain = gain_row(all_ref, gain_lane, 2 * size + mixed)
    for s in range(heads):
        normal, _ = norm_of(tok_refs[s][...].astype(F32))
        normed_ref[s * tok_rows : (s + 1) * tok_rows, :] = (normal * gain).astype(BF)
    pre = nn(normed_ref[...], all_ref[:, : 2 * size])
    cosine, sine = cos_ref[...], sin_ref[...]
    qkv_ref[:span, :size] = turn(pre[:, :size], cosine, sine).astype(BF)
    qkv_ref[:span, size : 2 * size] = turn(pre[:, size:], cosine, sine).astype(BF)
    extra = (qkv_ref.shape[0] - span) // (-(-heads // 3))
    for s in range(heads):
        rows = slice(span + s // 3 * extra, span + (s // 3 + 1) * extra)
        ids = ids_ref[head ^ s, ids_ref.shape[1] - extra :, :]
        qkv_ref[rows, s % 3 * LANES : (s % 3 + 1) * LANES] = ids
    for s in range(heads, -(-heads // 3) * 3):
        rows = slice(span + s // 3 * extra, span + (s // 3 + 1) * extra)
        qkv_ref[rows, s % 3 * LANES : (s % 3 + 1) * LANES] = jnp.zeros((extra, LANES), BF)
    wide = jnp.concatenate([ref[...] for ref in tok_refs])
    marks = []
    for s in range(heads):
        ids = ids_ref[head ^ s].astype(F32)
        ids = jnp.concatenate([ids, jnp.zeros((LANES - ids.shape[0], tok_rows), F32)])
        marks.append(ids.T.astype(BF))
    marks = jnp.concatenate(marks)
    row = lax.broadcasted_iota(jnp.int32, (LANES, LANES), 0)
    lane = lax.broadcasted_iota(jnp.int32, (LANES, LANES), 1)
    column = named * head_count + named * (head ^ (lane // att - 1))
    column = jnp.where(lane < att, named * head, column)
    valid = lane < att * (head_count + 1)
    expert = lax.broadcasted_iota(jnp.int32, (span, LANES), 1)
    inside = expert < att * (head_count + 1)
    expert = (expert % att).astype(F32)
    hot = jnp.zeros((span, LANES), F32)
    for k in range(named):
        ids = nn(marks, select(column + k, valid, row))
        hot = jnp.where(inside & (ids == expert), 1.0, hot)
    gates = jax.nn.sigmoid(nn(wide, all_ref[:, 2 * size + mixed :]))
    weight = hot * gates
    gate_ref[...] = gates
    weight_ref[...] = weight
    value = jnp.zeros((span, size), F32)
    first = 2 * size
    expert_values = nn(wide, all_ref[:, first : first + mixed])
    values_ref[...] = expert_values
    for e in range(att):
        value += weight[:, e : e + 1] * expert_values[:, e * size : (e + 1) * size]
    qkv_ref[:span, 2 * size :] = value.astype(BF)


def attend_kernel(groups, tok_rows, span, scale, at_ref, *refs):
    refs, (o_ref, lse_ref, top_ref, total_ref, acc_ref) = refs[:groups], refs[-5:]
    size = refs[0].shape[1] // 3
    blk, head = at_ref[0], at_ref[1]
    queries = refs[0][:span, :size]

    def advance(ref, first):
        scores = nt(ref[:span, size : 2 * size], queries) * scale
        if first:
            scores = jnp.where(own_allowed(blk, head, tok_rows, span), scores, -jnp.inf)
            top = jnp.max(scores, 0, keepdims=True)
        else:
            top = jnp.maximum(top_ref[...], jnp.max(scores, 0, keepdims=True))
        weights = jnp.exp(scores - top)
        mass = jnp.sum(weights, 0, keepdims=True)
        term = tn(ref[:span, 2 * size :], weights.astype(BF))
        if first:
            total_ref[...] = mass
            acc_ref[...] = term
        else:
            fade = jnp.exp(top_ref[...] - top)
            total_ref[...] = total_ref[...] * fade + mass
            acc_ref[...] = acc_ref[...] * fade + term
        top_ref[...] = top

    advance(refs[0], True)
    for mask in range(1, groups):
        pl.when((blk ^ mask) < blk)(functools.partial(advance, refs[mask], False))
    lse_ref[...] = top_ref[...] + jnp.log(total_ref[...])
    o_ref[...] = (acc_ref[...] / total_ref[...]).T.astype(BF)


def attend(at, qkv, tok_rows, span, scale, tokens):
    size = qkv[0].shape[1] // 3
    groups = len(qkv)
    return pl.pallas_call(
        functools.partial(attend_kernel, groups, tok_rows, span, scale),
        out_shape=(shape((span, size), BF), shape((1, span), F32)),
        in_specs=[SMEM] + [VMEM] * groups + [ANY] * len(tokens),
        out_specs=(VMEM, VMEM),
        scratch_shapes=[
            pltpu.VMEM((1, span), F32),
            pltpu.VMEM((1, span), F32),
            pltpu.VMEM((size, span), F32),
        ],
        compiler_params=PARAMS,
        cost_estimate=CHEAP,
        name="attend",
    )(at, *qkv, *tokens)


def attend_back_kernel(groups, tok_rows, span, scale, at_ref, *refs):
    own_refs, dout_refs = refs[:groups], refs[groups : 2 * groups]
    dq_ref, dk_ref, dv_ref, dq_acc = refs[-4:]
    size = own_refs[0].shape[1] // 3
    blk, head = at_ref[0], at_ref[1]
    parts = span // LANES

    def stat(ref, which):
        first = span + 2 * parts * which
        high = ref[first : first + parts, :].astype(F32)
        low = ref[first + parts : first + 2 * parts, :].astype(F32)
        both = high + low
        return jnp.concatenate([both[i : i + 1] for i in range(parts)], axis=1)

    def terms(key_ref, query_ref, dout_ref, own):
        scores = nt(key_ref[:span, size : 2 * size], query_ref[:span, :size]) * scale
        if own:
            scores = jnp.where(own_allowed(blk, head, tok_rows, span), scores, -jnp.inf)
        prob = jnp.exp(scores - stat(dout_ref, 0))
        prob_grad = nt(key_ref[:span, 2 * size :], dout_ref[:span, :])
        score_grad = prob * (prob_grad - stat(dout_ref, 1)) * scale
        return prob.astype(BF), score_grad.astype(BF)

    prob, grad = terms(own_refs[0], own_refs[0], dout_refs[0], True)
    dq_acc[...] = tn(own_refs[0][:span, size : 2 * size], grad)
    dk_ref[...] = nn(grad, own_refs[0][:span, :size])
    dv_ref[...] = nn(prob, dout_refs[0][:span, :])

    def earlier(mask):
        prob, grad = terms(own_refs[mask], own_refs[0], dout_refs[0], False)
        dq_acc[...] += tn(own_refs[mask][:span, size : 2 * size], grad)

    def later(mask):
        prob, grad = terms(own_refs[0], own_refs[mask], dout_refs[mask], False)
        dk_ref[...] += nn(grad, own_refs[mask][:span, :size])
        dv_ref[...] += nn(prob, dout_refs[mask][:span, :])

    for mask in range(1, groups):
        pl.when((blk ^ mask) < blk)(functools.partial(earlier, mask))
        pl.when((blk ^ mask) > blk)(functools.partial(later, mask))
    dq_ref[...] = dq_acc[...].T


def attend_back(at, qkv, douts, tok_rows, span, scale, tokens):
    size = qkv[0].shape[1] // 3
    groups = len(qkv)
    return pl.pallas_call(
        functools.partial(attend_back_kernel, groups, tok_rows, span, scale),
        out_shape=(shape((span, size), F32),) * 3,
        in_specs=[SMEM] + [VMEM] * (2 * groups) + [ANY] * len(tokens),
        out_specs=(VMEM,) * 3,
        scratch_shapes=[pltpu.VMEM((size, span), F32)],
        compiler_params=PARAMS,
        cost_estimate=CHEAP,
        name="attend_back",
    )(at, *qkv, *douts, *tokens)


def mix_kernel(layout, heads, at_ref, *refs):
    o_refs, tok_refs = refs[:heads], refs[heads : 2 * heads]
    weight_ref, wo_ref = refs[2 * heads : 2 * heads + 2]
    x1_ref, low_ref, high_ref, u_ref = refs[-4:]
    size, mixed, att, _, _ = layout
    head = at_ref[1]
    span = weight_ref.shape[0]
    tok_rows = span // heads

    @pl.when(pl.program_id(0) == 0)
    def _():
        for s in range(heads):
            start = (head ^ s) * mixed
            for r in range(heads):
                rows = slice(r * tok_rows, (r + 1) * tok_rows)
                there = slice((r ^ s) * tok_rows, ((r ^ s) + 1) * tok_rows)
                out = o_refs[s][there, :].astype(F32)
                for e in range(att):
                    lane = att + att * s + e
                    u_ref[rows, pl.ds(pl.multiple_of(start + e * size, size), size)] = (
                        weight_ref[rows, lane : lane + 1] * out
                    ).astype(BF)

    own = jnp.concatenate([ref[...] for ref in tok_refs]).astype(F32)
    x1 = own + nn(u_ref[...], wo_ref[...])
    x1_ref[...] = x1[:tok_rows]
    low = x1.astype(BF)
    low_ref[...] = low[: span // 2]
    high_ref[...] = low[span // 2 :]


def mix(layout, at, outs, tok_pieces, weight, w_output, tokens):
    heads = len(outs)
    span = weight.shape[0]
    depth, width = w_output.shape
    step = min(width, 256)

    def whole(array):
        return pl.BlockSpec(array.shape, lambda i: (0, 0))

    def columns(rows):
        return pl.BlockSpec((rows, step), lambda i: (0, i))

    return pl.pallas_call(
        functools.partial(mix_kernel, layout, heads),
        grid=(width // step,),
        out_shape=(
            shape((span // heads, width), F32),
            shape((span // 2, width), BF),
            shape((span // 2, width), BF),
            shape((span, depth), BF),
        ),
        in_specs=[SMEM]
        + [whole(o) for o in outs]
        + [columns(span // heads)] * heads
        + [whole(weight), columns(depth)]
        + [ANY] * len(tokens),
        out_specs=(
            columns(span // heads),
            columns(span // 2),
            columns(span // 2),
            pl.BlockSpec((span, depth), lambda i: (0, 0)),
        ),
        compiler_params=PARAMS,
        cost_estimate=CHEAP,
        name="mix",
    )(at, *outs, *tok_pieces, weight, w_output, *tokens)


SLOTS = 16


def sub_blocks(groups, heads, tok_rows):
    for p in range(groups):
        for s in range(heads):
            sub = p * heads + s
            rows = slice(s * tok_rows, (s + 1) * tok_rows)
            yield p, s, sub, rows, slice(sub * SLOTS, (sub + 1) * SLOTS)


def send_back(groups, heads, tok_rows, experts, slots, back, buf, targets, sems):
    sends = []
    width = buf.shape[2]
    for p, s, sub, rows, at in sub_blocks(groups, heads, tok_rows):
        values = slots[:experts, at, :].reshape(experts * SLOTS, width)
        buf[p, rows, :] = nn(back[sub], values).astype(BF)
        if s == heads - 1:
            move = pltpu.make_async_copy(buf.at[p], targets[p], sems.at[p])
            move.start()
            sends.append(move)
    return sends


def forward_kernel(plan, heads, experts, top, at_ref, *refs):
    chosen, count = plan
    groups = len(chosen)
    x_refs, id_refs = refs[:count], refs[count : count + groups]
    up_hbm, down_hbm, route_ref = refs[count + groups : count + groups + 3]
    outs = refs[count + groups + 3 :]
    out_refs = outs[:groups]
    xs_hbm, hidden_hbm, act_hbm, slope_hbm, here_hbm, back_hbm, gate_ref = outs[groups : groups + 7]
    xbuf, idbuf, xslot, hidden_ref, act_ref, slope_ref, up_ref, down_ref, here_ref, back = outs[
        groups + 7 : groups + 17
    ]
    in_sem, out_sem = outs[groups + 17 :]
    oslot = xbuf
    width = xbuf.shape[2]
    span = sum(x_refs[i].shape[0] for i in chosen[0])
    tok_rows = span // heads
    unit = up_ref.shape[1] // experts
    extra = idbuf.shape[1]
    arrivals = []
    sem = 0
    for p in range(groups):
        moves = []
        row = 0
        for index in chosen[p]:
            size = x_refs[index].shape[0]
            place = xbuf.at[p, pl.ds(row, size)]
            moves.append(pltpu.make_async_copy(x_refs[index], place, in_sem.at[sem]))
            row += size
            sem += 1
        source = id_refs[p].at[pl.ds(span, extra)]
        moves.append(pltpu.make_async_copy(source, idbuf.at[p], in_sem.at[sem]))
        sem += 1
        arrivals.append(moves)
    weights = [
        pltpu.make_async_copy(up_hbm, up_ref, in_sem.at[sem]),
        pltpu.make_async_copy(down_hbm, down_ref, in_sem.at[sem + 1]),
    ]
    for moves in [*arrivals, weights]:
        for move in moves:
            move.start()

    earlier = lax.broadcasted_iota(jnp.int32, (tok_rows, tok_rows), 0)
    later = lax.broadcasted_iota(jnp.int32, (tok_rows, tok_rows), 1)
    before = (earlier < later).astype(BF)
    place = lax.broadcasted_iota(jnp.int32, (experts, SLOTS, tok_rows), 1).astype(F32)
    for p, s, sub, rows, at in sub_blocks(groups, heads, tok_rows):
        if s == 0:
            for move in arrivals[p]:
                move.wait()
        ids = idbuf[p, s // 3 * top : (s // 3 + 1) * top, s % 3 * LANES : (s % 3 + 1) * LANES]
        ids = ids.astype(F32)
        hots = []
        for e in range(experts):
            met = ids == (at_ref[2] + e).astype(F32)
            hots.append(jnp.max(met.astype(F32), 0, keepdims=True))
        hot = jnp.concatenate(hots)
        rank = nn(hot.astype(BF), before)
        rank = jnp.where(hot > 0.0, rank, -1.0)
        here = (rank[:, None, :] == place).astype(F32).reshape(experts * SLOTS, tok_rows)
        back[sub] = here.T.astype(BF)
        here = here.astype(BF)
        here_ref[sub] = here
        moved = nn(here, xbuf[p, rows, :]).astype(BF)
        xslot[:experts, at, :] = moved.reshape(experts, SLOTS, width)
    saves = [
        pltpu.make_async_copy(source, target, out_sem.at[groups + i])
        for i, (source, target) in enumerate(
            (
                (xslot.at[pl.ds(0, experts)], xs_hbm),
                (here_ref, here_hbm),
                (back, back_hbm),
                (hidden_ref, hidden_hbm),
                (act_ref, act_hbm),
                (slope_ref, slope_hbm),
            )
        )
    ]
    for move in saves[:3]:
        move.start()
    for move in weights:
        move.wait()

    route = route_ref[...]
    held = xslot.shape[1]
    lane = lax.broadcasted_iota(jnp.int32, (held, LANES), 1)
    gate_slopes = jnp.zeros((held, LANES), F32)
    for e in range(experts):
        cols = slice(e * unit, (e + 1) * unit)
        both = jnp.concatenate([up_ref[:, cols], route], axis=1)
        pre_all = nn(xslot[e], both)
        pre, gate = pre_all[:, :unit], jax.nn.sigmoid(pre_all[:, unit + e : unit + e + 1])
        sig = jax.nn.sigmoid(pre)
        act = pre * sig
        hidden = (act * gate).astype(BF)
        hidden_ref[e] = hidden
        act_ref[e] = act
        slope_ref[e] = gate * (sig + act * (1.0 - sig))
        gate_slopes = jnp.where(lane == e, gate * (1.0 - gate), gate_slopes)
        oslot[e] = nn(hidden, down_ref[cols, :]).astype(BF)
    gate_ref[...] = gate_slopes
    for move in saves[3:]:
        move.start()
    saves[0].wait()
    sends = send_back(
        groups, heads, tok_rows, experts, oslot, back, xslot, out_refs, out_sem
    )
    for move in [*saves[1:], *sends]:
        move.wait()


def back_kernel(far, groups, heads, experts, at_ref, *refs):
    g_hbm, up_hbm, down_hbm, act_hbm, slope_hbm, here_hbm, back_hbm = refs[:7]
    route_ref, gate_ref = refs[7:9]
    dx_refs, (gs_hbm, da_ref) = refs[9 : 9 + groups], refs[9 + groups : 11 + groups]
    gbuf, gslot, dslot, act_ref, slope_ref, up_ref, down_ref, here_ref, back = refs[
        11 + groups : 20 + groups
    ]
    in_sem, out_sem = refs[20 + groups :]
    tok_rows, width = gbuf.shape[2:]
    unit = up_ref.shape[1] // experts
    arrivals = [
        [
            pltpu.make_async_copy(source, target, in_sem.at[i])
            for i, (source, target) in enumerate(
                (
                    (here_hbm, here_ref),
                    (down_hbm, down_ref),
                    (act_hbm, act_ref),
                    (slope_hbm, slope_ref),
                    (up_hbm, up_ref),
                    (back_hbm, back),
                )
            )
        ]
    ]
    sem = len(arrivals[0])
    for p in range(groups):
        moves = []
        for s in range(heads):
            device = (at_ref[0] ^ (far + p)) * heads + (at_ref[1] ^ s)
            source = g_hbm.at[pl.ds(pl.multiple_of(device * tok_rows, tok_rows), tok_rows)]
            moves.append(pltpu.make_async_copy(source, gbuf.at[p, s], in_sem.at[sem]))
            sem += 1
        arrivals.append(moves)
    arrivals[0][0].start()
    for moves in arrivals[1:]:
        for move in moves:
            move.start()
    for move in arrivals[0][1:]:
        move.start()
    arrivals[0][0].wait()
    for p, s, sub, rows, at in sub_blocks(groups, heads, tok_rows):
        if s == 0:
            for move in arrivals[1 + p]:
                move.wait()
        moved = nn(here_ref[sub], gbuf[p, s]).astype(BF)
        gslot[:experts, at, :] = moved.reshape(experts, SLOTS, width)
    save = pltpu.make_async_copy(gslot.at[pl.ds(0, experts)], gs_hbm, out_sem.at[groups])
    save.start()
    for move in arrivals[0][1:]:
        move.wait()
    route = route_ref[...]
    held = gslot.shape[1]
    lane = lax.broadcasted_iota(jnp.int32, (held, LANES), 1)
    for e in range(experts):
        cols = slice(e * unit, (e + 1) * unit)
        both = jnp.concatenate([up_ref[:, cols], route], axis=1)
        dh = nt(gslot[e], down_ref[cols, :])
        da = (dh * slope_ref[e]).astype(BF)
        dsm = jnp.sum(dh * act_ref[e], -1, keepdims=True) * gate_ref[...]
        dsm = jnp.where(lane == e, dsm, 0.0).astype(BF)
        da = jnp.concatenate([da, dsm], axis=1)
        da_ref[e] = da
        dslot[e] = nt(da, both).astype(BF)
    save.wait()
    sends = send_back(groups, heads, tok_rows, experts, dslot, back, gslot, dx_refs, out_sem)
    for move in sends:
        move.wait()


def run_experts(at, far, xs, ids, g_all, up, down, route, experts, top, heads):
    groups = len(xs)
    width, units = up.shape
    unit = units // experts
    span = sum(x.shape[0] for x in xs[0])
    tok_rows = span // heads
    held = groups * heads * SLOTS
    chosen, flat = [], []
    for arrays in xs:
        chosen.append(tuple(range(len(flat), len(flat) + len(arrays))))
        flat += arrays
    subs = groups * heads
    slots = pltpu.VMEM((max(experts, groups), max(held, span), width), BF)
    dims = {
        "rows": ((experts, held, width), BF),
        "hidden": ((experts, held, unit), BF),
        "wide": ((experts, held, unit), F32),
        "here": ((subs, experts * SLOTS, tok_rows), BF),
        "back": ((subs, tok_rows, experts * SLOTS), BF),
    }
    vm = {name: pltpu.VMEM(*dim) for name, dim in dims.items()}
    hbm = {name: shape(*dim) for name, dim in dims.items()}
    both = [pltpu.VMEM((width, units), BF), pltpu.VMEM((units, width), BF)]
    params = pltpu.CompilerParams(vmem_limit_bytes=58 * MIB)
    done = pl.pallas_call(
        functools.partial(forward_kernel, (chosen, len(flat)), heads, experts, top),
        out_shape=(shape((span, width), BF),) * groups
        + (hbm["rows"], hbm["hidden"], hbm["wide"], hbm["wide"], hbm["here"], hbm["back"])
        + (shape((held, LANES), F32),),
        in_specs=[SMEM] + [ANY] * (len(flat) + groups + 2) + [VMEM],
        out_specs=(ANY,) * (groups + 6) + (VMEM,),
        scratch_shapes=[
            slots,
            pltpu.VMEM((groups, ids[0].shape[0] - span, ids[0].shape[1]), BF),
            slots,
            vm["hidden"],
            vm["wide"],
            vm["wide"],
            *both,
            vm["here"],
            vm["back"],
            pltpu.SemaphoreType.DMA((len(flat) + groups + 2,)),
            pltpu.SemaphoreType.DMA((groups + 6,)),
        ],
        compiler_params=params,
        cost_estimate=CHEAP,
        name="experts_forward",
    )(at, *flat, *ids, up, down, route)
    outs, (rows, hidden, act, slope, here, back, gates) = done[:groups], done[groups:]
    done = pl.pallas_call(
        functools.partial(back_kernel, far, groups, heads, experts),
        out_shape=(shape((span, width), BF),) * groups
        + (hbm["rows"], shape((experts, held, unit + LANES), BF)),
        in_specs=[SMEM] + [ANY] * 7 + [VMEM, VMEM],
        out_specs=(ANY,) * (groups + 1) + (VMEM,),
        scratch_shapes=[
            pltpu.VMEM((groups, heads, tok_rows, width), BF),
            slots,
            vm["rows"],
            vm["wide"],
            vm["wide"],
            *both,
            vm["here"],
            vm["back"],
            pltpu.SemaphoreType.DMA((6 + subs,)),
            pltpu.SemaphoreType.DMA((groups + 1,)),
        ],
        compiler_params=params,
        cost_estimate=CHEAP,
        name="experts_back",
    )(at, g_all, up, down, act, slope, here, back, route, gates)
    return outs, done[:groups], (rows, done[groups], hidden, done[groups + 1])


def expert_grads_kernel(halves, *refs):
    x_refs, g_refs, hidden_refs, da_refs = (
        refs[i * halves : (i + 1) * halves] for i in range(4)
    )
    up_ref, down_ref, route_ref = refs[-3:]
    unit = up_ref.shape[1]
    up = down = None
    for x_ref, g_ref, hidden_ref, da_ref in zip(x_refs, g_refs, hidden_refs, da_refs):
        term = tn(x_ref[0], da_ref[0])
        up = term if up is None else up + term
        term = tn(hidden_ref[0], g_ref[0])
        down = term if down is None else down + term
    up_ref[...] = up[:, :unit]
    down_ref[...] = down

    @pl.when(pl.program_id(0) == 0)
    def _():
        route_ref[...] = up[:, unit:]

    @pl.when(pl.program_id(0) > 0)
    def _():
        route_ref[...] += up[:, unit:]


def expert_grads(results, tokens):
    halves = len(results)
    experts, held, width = results[0][0].shape
    unit = results[0][2].shape[2]

    def block(array):
        return pl.BlockSpec((1,) + array.shape[1:], lambda e: (e, 0, 0))

    flat = [result[i] for i in range(4) for result in results]
    return pl.pallas_call(
        functools.partial(expert_grads_kernel, halves),
        grid=(experts,),
        out_shape=(
            shape((width, experts * unit), F32),
            shape((experts * unit, width), F32),
            shape((width, LANES), F32),
        ),
        in_specs=[block(array) for array in flat] + [ANY] * len(tokens),
        out_specs=(
            pl.BlockSpec((width, unit), lambda e: (0, e)),
            pl.BlockSpec((unit, width), lambda e: (e, 0)),
            pl.BlockSpec((width, LANES), lambda e: (0, 0)),
        ),
        compiler_params=PARAMS,
        cost_estimate=CHEAP,
        name="expert_grads",
    )(*flat, *tokens)


def spread_kernel(layout, heads, terms, at_ref, *refs):
    term_refs = refs[:terms]
    grad_ref, wo_ref, weight_ref = refs[terms : terms + 3]
    o_refs = refs[terms + 3 : terms + 3 + heads]
    g1_ref, low_ref = refs[-2 - heads : -heads]
    send_refs = refs[-heads:]
    size, mixed, att, _, _ = layout
    head = at_ref[1]
    span = g1_ref.shape[0]
    tok_rows = span // heads
    total = term_refs[0][...].astype(F32)
    for ref in term_refs[1:]:
        total += ref[...].astype(F32)
    g1_ref[...] = total
    g1_ref[:tok_rows, :] += grad_ref[...].astype(F32)
    low_ref[...] = g1_ref[...].astype(BF)
    lane = lax.broadcasted_iota(jnp.int32, (tok_rows, LANES), 1)
    for s in range(heads):
        start = pl.multiple_of((head ^ s) * mixed, LANES)
        du = nt(low_ref[...], wo_ref[pl.ds(start, mixed), :])
        for r in range(heads):
            rows = slice(r * tok_rows, (r + 1) * tok_rows)
            there = slice((r ^ s) * tok_rows, ((r ^ s) + 1) * tok_rows)
            out = o_refs[s][there, :].astype(F32)
            dout = jnp.zeros((tok_rows, size), F32)
            dots = jnp.zeros((tok_rows, LANES), F32)
            for e in range(att):
                at = att + att * s + e
                term = du[rows, e * size : (e + 1) * size]
                dout += weight_ref[rows, at : at + 1] * term
                dots = jnp.where(lane == e, jnp.sum(term * out, -1, keepdims=True), dots)
            send_refs[s][there, :] = dout.astype(BF)
            high, low = high_low(dots.T[:8, :])
            first = span + 16 * (r ^ s)
            send_refs[s][first : first + 16, :] = jnp.concatenate([high, low])


def spread(layout, at, terms, out_grad, w_output, weight, outs, tokens):
    heads = len(outs)
    span, width = terms[0].shape
    tok_rows = span // heads
    size = outs[0].shape[1]
    return pl.pallas_call(
        functools.partial(spread_kernel, layout, heads, len(terms)),
        out_shape=(shape((span, width), F32), shape((span, width), BF))
        + (shape((span + 16 * heads, size), BF),) * heads,
        in_specs=[SMEM] + [VMEM] * (len(terms) + 3 + heads) + [ANY] * len(tokens),
        out_specs=(VMEM,) * (2 + heads),
        compiler_params=PARAMS,
        cost_estimate=CHEAP,
        name="spread",
    )(at, *terms, out_grad, w_output, weight, *outs, *tokens)


def join_kernel(heads, att, *refs):
    got_refs, (o_ref, lse_ref, gate_ref, weight_ref) = refs[:heads], refs[heads : heads + 4]
    dout_ref, dso_ref = refs[-2:]
    span, size = o_ref.shape
    tok_rows = span // heads
    parts = span // LANES
    total = got_refs[0][...].astype(F32)
    for ref in got_refs[1:]:
        total += ref[...].astype(F32)
    low = total[:span].astype(BF)
    dout_ref[:span, :] = low
    product = low.astype(F32) * o_ref[...].astype(F32)
    stats = []
    lse = lse_ref[...]
    rows = [lse[:, i * LANES : (i + 1) * LANES] for i in range(parts)]
    stats += high_low(jnp.concatenate(rows))
    rows = [
        jnp.sum(product[i * LANES : (i + 1) * LANES].T, 0, keepdims=True) for i in range(parts)
    ]
    stats += high_low(jnp.concatenate(rows))
    dout_ref[span:, :] = jnp.concatenate(stats)
    for r in range(heads):
        first = span + 16 * r
        sums = total[first : first + 8] + total[first + 8 : first + 16]
        sums = jnp.concatenate([sums, jnp.zeros((LANES - 8, LANES), F32)]).T
        rows = slice(r * tok_rows, (r + 1) * tok_rows)
        moved = pltpu.roll(sums, att, 1)
        dso_ref[rows, :] = (moved * weight_ref[rows, :] * (1.0 - gate_ref[rows, :])).astype(BF)


def join(got, mine, log_total, gate, weight, att, tokens):
    heads = len(got)
    span, size = mine.shape
    parts = span // LANES
    return pl.pallas_call(
        functools.partial(join_kernel, heads, att),
        out_shape=(shape((span + 4 * parts, size), BF), shape((span, LANES), BF)),
        in_specs=[VMEM] * (heads + 4) + [ANY] * len(tokens),
        out_specs=(VMEM, VMEM),
        compiler_params=PARAMS,
        cost_estimate=CHEAP,
        name="join",
    )(*got, mine, log_total, gate, weight, *tokens)


def output_grad_kernel(rows, groups, at_ref, u_ref, g_ref, even_ref, odd_ref, all_ref):
    all_ref[...] = tn(u_ref[...], g_ref[...]).astype(BF)
    for mask in range(groups):
        place = pl.ds(pl.multiple_of((at_ref[0] ^ mask) * rows, rows), rows)
        ref = odd_ref if mask % 2 else even_ref
        ref[mask // 2 * rows : (mask // 2 + 1) * rows, :] = all_ref[place, :]


def output_grad(at, u, g, groups):
    depth, width = u.shape[1], g.shape[1]
    half = shape((depth // 2, width), BF)
    return pl.pallas_call(
        functools.partial(output_grad_kernel, depth // groups, groups),
        out_shape=(half, half),
        in_specs=[SMEM, VMEM, VMEM],
        out_specs=(VMEM, VMEM),
        scratch_shapes=[pltpu.VMEM((depth, width), BF)],
        compiler_params=PARAMS,
        cost_estimate=CHEAP,
        name="output_grad",
    )(at, u, g)


def pair_kernel(mine_ref, got_ref, *refs):
    rows = refs[0].shape[0]
    for i, ref in enumerate(refs):
        at = slice(i * rows, (i + 1) * rows)
        total = mine_ref[at, :].astype(F32) + got_ref[at, :].astype(F32)
        ref[...] = total.astype(ref.dtype)


def pair_rows(mine, got, parts):
    rows = (mine.shape[0] // parts, mine.shape[1])
    return pl.pallas_call(
        pair_kernel,
        out_shape=(shape(rows, F32),) + (shape(rows, BF),) * (parts - 1),
        in_specs=[VMEM, VMEM],
        out_specs=(VMEM,) * parts,
        compiler_params=PARAMS,
        cost_estimate=CHEAP,
        name="pair_rows",
    )(mine, got)


def unpack_kernel(layout, all_ref, q_ref, k_ref, v_ref, rv_ref, ro_ref, gain_ref):
    size, mixed, att, head_count, gain_lane = layout
    row = lax.broadcasted_iota(jnp.int32, (LANES, LANES), 0)
    lane = lax.broadcasted_iota(jnp.int32, (LANES, LANES), 1)
    few = att * head_count
    values = outputs = gains = None
    for h in range(head_count):
        q_ref[:, h * size : (h + 1) * size] = all_ref[h, :, :size].astype(F32)
        k_ref[:, h * size : (h + 1) * size] = all_ref[h, :, size : 2 * size].astype(F32)
        v_ref[:, h * mixed : (h + 1) * mixed] = all_ref[h, :, 2 * size : 2 * size + mixed].astype(
            F32
        )
        tail = all_ref[h, :, 2 * size + mixed :]
        here = (row >= att * h) & (row < att * (h + 1))
        value = nt(select(row - att * h, here, lane), tail)
        output = nt(select(row - att * h + att, here, lane), tail)
        gain = nt((lane == gain_lane).astype(BF), tail)
        values = value if h == 0 else values + value
        outputs = output if h == 0 else outputs + output
        gains = gain if h == 0 else gains + gain
    rv_ref[...] = values[:few]
    ro_ref[...] = outputs[:few]
    gain_ref[...] = gains[:1]


def branch_kernel(heads, *refs):
    x1_ref, own_ref, send_refs = refs[0], refs[-heads], refs[1 - heads :]
    rows = x1_ref.shape[0]
    for s in range(heads):
        at = slice(s * rows, (s + 1) * rows)
        total = sum(ref[at, :].astype(F32) for ref in refs[1:-heads])
        if s == 0:
            own_ref[...] = x1_ref[...] + total
        else:
            send_refs[s - 1][...] = total.astype(BF)


def branch(x1, terms, heads):
    return pl.pallas_call(
        functools.partial(branch_kernel, heads),
        out_shape=(shape(x1.shape, F32),) + (shape(x1.shape, BF),) * (heads - 1),
        in_specs=[VMEM] * (1 + len(terms)),
        out_specs=(VMEM,) * heads,
        compiler_params=PARAMS,
        cost_estimate=CHEAP,
        name="branch",
    )(x1, *terms)


def finish_kernel(layout, heads, groups, at_ref, *refs):
    (
        dq_ref, dk_ref, dv_ref, cos_ref, sin_ref, values_ref, gate_ref, weight_ref, dso_ref,
        normed_ref, all_ref, g1_ref,
    ) = refs[:12]
    tok_refs = refs[12 : 12 + heads]
    part_refs = refs[-4 - heads : -4]
    even_ref, odd_ref, product_ref, all_grads = refs[-4:]
    size, mixed, att, _, gain_lane = layout
    blk = at_ref[0]
    span, width = normed_ref.shape
    tok_rows = span // heads
    cosine, sine = cos_ref[...], -sin_ref[...]
    query_back = turn(dq_ref[...], cosine, sine).astype(BF)
    key_back = turn(dk_ref[...], cosine, sine).astype(BF)
    qk_back = jnp.concatenate([query_back, key_back], axis=1)
    value_back = dv_ref[...].astype(BF).astype(F32)
    lane = lax.broadcasted_iota(jnp.int32, (span, LANES), 1)
    dots = jnp.zeros((span, LANES), F32)
    columns = []
    for e in range(att):
        columns.append((weight_ref[:, e : e + 1] * value_back).astype(BF))
        dot = jnp.sum(value_back * values_ref[:, e * size : (e + 1) * size], -1, keepdims=True)
        dots = jnp.where(lane == e, dot, dots)
    gates = gate_ref[...]
    tail = (dots * weight_ref[...] * (1.0 - gates)).astype(BF)
    tail = jnp.where(lane < att, tail, jnp.where(lane < 2 * att, dso_ref[...], jnp.zeros_like(tail)))
    v_back = jnp.concatenate(columns + [tail], axis=1)
    gain = gain_row(all_ref, gain_lane, 2 * size + mixed)
    grad_normed = nt(qk_back, all_ref[:, : 2 * size])
    grad_wide = nt(v_back, all_ref[:, 2 * size :])
    for s in range(heads):
        rows = slice(s * tok_rows, (s + 1) * tok_rows)
        normal, inv_std = norm_of(tok_refs[s][...].astype(F32))
        product_ref[rows, :] = (grad_normed[rows] * normal).astype(BF)
        grad_normal = grad_normed[rows] * gain
        part = (
            g1_ref[rows, :]
            + grad_wide[rows]
            + inv_std
            * (
                grad_normal
                - jnp.mean(grad_normal, -1, keepdims=True)
                - normal * jnp.mean(grad_normal * normal, -1, keepdims=True)
            )
        )
        part_refs[s][...] = part if s == 0 else part.astype(BF)
    own = width // groups
    gain_pick = (lane == gain_lane).astype(BF)
    wide = jnp.concatenate([ref[...] for ref in tok_refs])
    all_grads[:, : 2 * size] = tn(normed_ref[...], qk_back).astype(BF)
    from_tokens = tn(wide, v_back)
    all_grads[:, 2 * size : 2 * size + mixed] = from_tokens[:, :mixed].astype(BF)
    all_grads[:, 2 * size + mixed :] = (
        from_tokens[:, mixed:] + tn(product_ref[...], gain_pick)
    ).astype(BF)
    for mask in range(groups):
        place = pl.ds(pl.multiple_of((blk ^ mask) * own, own), own)
        ref = odd_ref if mask % 2 else even_ref
        ref[mask // 2 * own : (mask // 2 + 1) * own, :] = all_grads[place, :]


def finish(layout, heads, groups, at, tokens, *arrays):
    span, width = arrays[9].shape
    packed = arrays[10].shape[1]
    half = (width // 2, packed)
    return pl.pallas_call(
        functools.partial(finish_kernel, layout, heads, groups),
        out_shape=(shape((span // heads, width), F32),)
        + (shape((span // heads, width), BF),) * (heads - 1)
        + (shape(half, BF), shape(half, BF)),
        in_specs=[SMEM] + [VMEM] * len(arrays) + [ANY] * len(tokens),
        out_specs=(VMEM,) * (heads + 2),
        scratch_shapes=[pltpu.VMEM((span, width), BF), pltpu.VMEM((width, packed), BF)],
        compiler_params=PARAMS,
        cost_estimate=CHEAP,
        name="finish",
    )(at, *arrays, *tokens)


def on_device(
    tokens,
    out_grad,
    ln_gain,
    w_query,
    w_key,
    w_value,
    w_output,
    route_value,
    route_output,
    route_expert,
    w_up,
    w_down,
    value_ids,
    output_ids,
    expert_ids,
):
    groups, heads = lax.axis_size("blk"), lax.axis_size("head")
    blk, head = lax.axis_index("blk"), lax.axis_index("head")
    tok_rows, width = tokens.shape
    head_count, named = value_ids.shape[1:]
    att = route_value.shape[1] // head_count
    size = w_query.shape[1] // head_count
    experts = route_expert.shape[1]
    top = expert_ids.shape[1]
    span = tok_rows * heads
    own_rows = w_query.shape[0]
    mixed = att * size
    scale = size ** (-0.5)
    device = blk * heads + head
    at = jnp.stack([blk, head, device * experts]).astype(jnp.int32)
    gain_lane = att + head_count * att
    layout = (size, mixed, att, head_count, gain_lane)
    used = 2 * size + mixed + gain_lane + 1
    packed = 2 * size + mixed + LANES

    ids_rows = 2 * named * head_count + top
    ids = jnp.concatenate(
        [
            value_ids.transpose(1, 2, 0).reshape(-1, tok_rows),
            output_ids.transpose(1, 2, 0).reshape(-1, tok_rows),
            expert_ids.T,
        ]
    )
    by_head, second, third = pl.pallas_call(
        functools.partial(pack_kernel, layout),
        out_shape=(
            shape((head_count, max(own_rows, ids_rows), packed + tok_rows), BF),
            shape(tokens.shape, BF),
            shape(tokens.shape, BF),
        ),
        in_specs=[VMEM] * 8,
        out_specs=(VMEM,) * 3,
        compiler_params=PARAMS,
        name="pack",
    )(w_query, w_key, w_value, route_value.T, route_output.T, ln_gain[None], ids, tokens)
    tok_pieces = [tokens, swap(tokens, "head", 1)]
    by_head = lax.all_to_all(by_head, "head", 0, 0, tiled=True)
    third = hold(third, by_head)
    for mask in range(2, heads):
        tok_pieces.append(swap(second if mask == 2 else third, "head", mask))
    ids_group = by_head[:, :ids_rows, packed:]
    w_pieces = gather_blk(by_head[:, :own_rows, :packed].reshape(heads * own_rows, packed))

    wo_full = lax.all_gather(w_output, ("blk", "head"), axis=0, tiled=True)

    places = jnp.arange(span)
    places = blk * span + (head ^ (places // tok_rows)) * tok_rows + places % tok_rows
    half = size // 2
    frequency = rope_base ** (-jnp.arange(half, dtype=F32) / half)
    angles = places.astype(F32)[:, None] * frequency[None, :]
    cosine, sine = jnp.cos(angles), jnp.sin(angles)
    cosine = jnp.concatenate([cosine, cosine], axis=1)
    sine = jnp.concatenate([-sine, sine], axis=1)

    qkv, expert_values, gate, weight, weights, normed = pl.pallas_call(
        functools.partial(project_kernel, layout, heads, groups, named),
        out_shape=(
            shape((span + -(-heads // 3) * top, 3 * size), BF),
            shape((span, mixed), F32),
            shape((span, LANES), F32),
            shape((span, LANES), F32),
            shape((width, packed), BF),
            shape((span, width), BF),
        ),
        in_specs=[SMEM] + [VMEM] * (3 + heads + groups),
        out_specs=(VMEM,) * 6,
        compiler_params=PARAMS,
        cost_estimate=CHEAP,
        name="project",
    )(at, cosine, sine, ids_group, *tok_pieces, *w_pieces)

    g_all = lax.all_gather(hold(out_grad, qkv), ("blk", "head"), axis=0, tiled=True)

    qkv_pieces = gather_blk(qkv)
    mine, log_total = attend(at, qkv_pieces, tok_rows, span, scale, [])
    outs = gather_head(mine)
    x1, *middle, mixed_heads = mix(layout, at, outs, tok_pieces, weight, wo_full, [])

    route = jnp.pad(route_expert, ((0, 0), (0, LANES - experts)))
    near = 8
    branch_terms = grad_terms = weight_grads = None

    def pair_sum(parts, mask):
        return add_low(parts[mask], swap(parts[mask + 1], "blk", 1))

    for far in range(0, groups, near):
        base = middle
        if far:
            base, *old = lax.optimization_barrier(
                (base, branch_terms, grad_terms, *weight_grads)
            )
            branch_terms, grad_terms, *weight_grads = old
            base = [swap(rows, "blk", far) for rows in base]
        even = {0: base}
        for mask in (2, 4):
            even[mask] = [swap(rows, "blk", mask) for rows in base]
        even[6] = [swap(even[2][0], "blk", 4), swap(even[4][1], "blk", 2)]
        xs = []
        for mask in range(0, near, 2):
            xs += [even[mask], [swap(x, "blk", 1) for x in even[mask]]]
        outs_all, dxs_all, saved = run_experts(
            at, far, xs, qkv_pieces[far : far + near], g_all, w_up, w_down, route,
            experts, top, heads,
        )
        sums = [pair_sum(dxs_all, m) for m in (2, 4, 6)]
        grad_round = [dxs_all[0], swap(dxs_all[1], "blk", 1)]
        grad_round += [swap(value, "blk", m) for m, value in zip((2, 4, 6), sums)]
        terms = expert_grads([saved], sums)
        out_sums = [hold(pair_sum(outs_all, m), sums[-1]) for m in (2, 4, 6)]
        branch_round = [outs_all[0], swap(outs_all[1], "blk", 1)]
        out_sums = [hold(value, grad_round[-1]) for value in out_sums]
        branch_round += [swap(value, "blk", m) for m, value in zip((2, 4, 6), out_sums)]
        if groups > near:
            def whole(terms):
                return functools.reduce(lambda a, b: a + b, [t.astype(F32) for t in terms])

            out_sum, dx_sum = whole(branch_round), whole(grad_round)
            if far:
                out_sum = branch_terms + swap(out_sum.astype(BF), "blk", far).astype(F32)
                dx_sum = grad_terms + swap(dx_sum.astype(BF), "blk", far).astype(F32)
                weight_grads = [old + new for old, new in zip(weight_grads, terms)]
            else:
                weight_grads = terms
            branch_terms, grad_terms = out_sum, dx_sum
        else:
            branch_terms, grad_terms, weight_grads = branch_round, grad_round, terms
    early = [*out_sums, weight_grads[2]]
    arrived = branch_round[2:]
    if groups > near:
        branch_terms, grad_terms = [branch_terms], [grad_terms]
    grad_up, grad_down, grad_route_expert = weight_grads
    grad_route_expert = grad_route_expert[:, :experts]

    g1, g1_low, *sends = spread(layout, at, grad_terms, out_grad, wo_full, weight, outs, early)
    even, odd = output_grad(at, mixed_heads, g1_low, groups)
    got = [sends[0]] + [swap(sends[m], "head", m) for m in range(1, heads)]
    dout, dso = join(got, mine, log_total, gate, weight, att, [odd])
    dout_pieces = gather_blk(hold(dout, *arrived[:2]))
    layer_out, *outputs = branch(x1, branch_terms, heads)
    pair_sums = pair_rows(even, swap(hold(odd, *arrived), "blk", 1), groups // 2)
    pair_sums = [hold(rows, *dout_pieces) for rows in pair_sums]
    dq, dk, dv = attend_back(
        at, qkv_pieces, dout_pieces, tok_rows, span, scale, [outputs[0], pair_sums[0]]
    )

    out_rows = w_output.shape[0]
    there, last_rows = [], []
    rows_sum = pair_sums[0]
    for index in range(1, groups // 2):
        got_rows = swap(pair_sums[index], "blk", 2 * index)
        there.append(got_rows)
        rows_sum = rows_sum + got_rows.astype(F32)
    rows_sum = rows_sum.reshape(heads, out_rows, width)
    grad_output = lax.dynamic_index_in_dim(rows_sum, head, 0, keepdims=False)
    for mask in range(1, heads):
        sent = lax.dynamic_index_in_dim(rows_sum, head ^ mask, 0, keepdims=False).astype(BF)
        there.append(sent)
        last_rows.append(swap(sent, "head", mask))
        grad_output = grad_output + last_rows[-1].astype(F32)
        got_rows = swap(outputs[mask - 1], "head", mask)
        there.append(got_rows)
        layer_out = layer_out + got_rows.astype(F32)

    grad_input, *parts, even_rows, odd_rows = finish(
        layout, heads, groups, at, there, dq, dk, dv, cosine, sine, expert_values, gate, weight, dso,
        normed, weights, g1, *tok_pieces,
    )
    parts = [hold(rows, *last_rows) for rows in parts]
    summed, *pairs = pair_rows(even_rows, swap(odd_rows, "blk", 1), groups // 2)
    for index, piece in enumerate(pairs):
        summed = summed + swap(piece, "blk", 2 * index + 2).astype(F32)
    for mask in range(1, heads):
        grad_input = grad_input + swap(parts[mask - 1], "head", mask).astype(F32)
    summed = lax.all_to_all(
        summed.astype(BF).reshape(heads, own_rows, packed), "head", 0, 0, tiled=True
    )
    few = head_count * att
    full = [(own_rows, head_count * columns) for columns in (size, size, mixed)]
    flat = [(few, own_rows), (few, own_rows), (1, own_rows)]
    grad_query, grad_key, grad_value, *routers, grad_gain = pl.pallas_call(
        functools.partial(unpack_kernel, layout),
        out_shape=tuple(shape(dims, F32) for dims in full + flat),
        in_specs=[VMEM],
        out_specs=(VMEM,) * 6,
        compiler_params=PARAMS,
        cost_estimate=CHEAP,
        name="unpack",
    )(summed)
    grad_value_router, grad_output_router = (rows.T for rows in routers)
    grad_gain = grad_gain[0]

    return (
        layer_out,
        grad_input,
        grad_gain,
        grad_query,
        grad_key,
        grad_value,
        grad_output,
        grad_value_router,
        grad_output_router,
        grad_route_expert,
        grad_up,
        grad_down,
    )


def solution(mesh):
    both = P(("blk", "head"), None)
    columns = P(None, ("blk", "head"))
    vector = P(("blk", "head"))
    triple = P(("blk", "head"), None, None)
    return jax.shard_map(
        on_device,
        mesh=mesh,
        in_specs=(
            both, both, vector, both, both, both, both, both, both, columns, columns, both,
            triple, triple, both,
        ),
        out_specs=(
            both, both, vector, both, both, both, both, both, both, columns, columns, both,
        ),
        check_vma=False,
    )
```
